32 devices in a mesh: head: 4 (over x, core), blk: 8 (over z, y).
Axes of the slice: x: 2, y: 2, z: 4, core: 2. Of those that a mesh axis runs over, the one named last changes fastest.
Arguments:
- tokens_in: bfloat16 [8, 4096, 768], P('blk', 'head'), may hold values from -6 to 6
- query_weight: float32 [768, 768], P(('head', 'blk')), may hold values from -0.21875 to 0.21875
- query_bias: float32 [768], P(('head', 'blk')), may hold values from -3 to 3
- key_weight: float32 [768, 768], P(('head', 'blk')), may hold values from -0.21875 to 0.21875
- value_weight: float32 [768, 768], P(('head', 'blk')), may hold values from -0.21875 to 0.21875
- value_bias: float32 [768], P(('head', 'blk')), may hold values from -3 to 3
- mixer_weight: float32 [768, 768], P(('head', 'blk')), may hold values from -3.5 to 3.5
- mixer_bias: float32 [768], P(('head', 'blk')), may hold values from -2 to 2
- first_gain: float32 [768], P(('head', 'blk')), may hold values from 0.5 to 1.5
- first_shift: float32 [768], P(('head', 'blk')), may hold values from -2 to 2
- expand_weight: float32 [768, 3072], P(('head', 'blk')), may hold values from -0.21875 to 0.21875
- expand_bias: float32 [3072], P(('head', 'blk')), may hold values from -3 to 3
- shrink_weight: float32 [3072, 768], P(('head', 'blk')), may hold values from -0.109375 to 0.109375
- shrink_bias: float32 [768], P(('head', 'blk')), may hold values from -2 to 2
- second_gain: float32 [768], P(('head', 'blk')), may hold values from 0.5 to 1.5
- second_shift: float32 [768], P(('head', 'blk')), may hold values from -2 to 2
- doc_starts: int32 [12], replicated, may hold values from 0 to 32767, as said below
- random_blocks: int32 [512, 3], P('blk'), may hold values from 0 to 511, as said below
- cotangent: bfloat16 [8, 4096, 768], P('blk', 'head'), may hold values from -6 to 6
Outputs:
- layer_out: bfloat16 [8, 4096, 768], P('blk', 'head')
- input_grad: float32 [8, 4096, 768], P('blk', 'head')
- query_weight_grad: float32 [768, 768], P(('head', 'blk'))
- query_bias_grad: float32 [768], P(('head', 'blk'))
- key_weight_grad: float32 [768, 768], P(('head', 'blk'))
- value_weight_grad: float32 [768, 768], P(('head', 'blk'))
- value_bias_grad: float32 [768], P(('head', 'blk'))
- mixer_weight_grad: float32 [768, 768], P(('head', 'blk'))
- mixer_bias_grad: float32 [768], P(('head', 'blk'))
- first_gain_grad: float32 [768], P(('head', 'blk'))
- first_shift_grad: float32 [768], P(('head', 'blk'))
- expand_weight_grad: float32 [768, 3072], P(('head', 'blk'))
- expand_bias_grad: float32 [3072], P(('head', 'blk'))
- shrink_weight_grad: float32 [3072, 768], P(('head', 'blk'))
- shrink_bias_grad: float32 [768], P(('head', 'blk'))
- second_gain_grad: float32 [768], P(('head', 'blk'))
- second_shift_grad: float32 [768], P(('head', 'blk'))
The draws below stay inside these ranges and needn't reach their ends.
Inputs may be any that keep to these rules, and one draw needn't show every extreme that they name: Increasing, doc_starts[0] = 0; a document runs from its start to the next start, the last one to 32768; every document holds between 1365 and 4096 tokens, and one holds exactly 4096. `random_blocks`: each entry of row j is a block holding some token of the document of position 64 * j; entries may repeat.
All inputs are finite; a program needn't handle non-finite values.
Results may differ from the reference program's by a relative error of at most 0.014.
The reference program's roundings to bfloat16 on the way count: a program that leaves them out, or rounds other values in their place, can miss the bound.
Values may be sent and summed in bfloat16 or wider, within the bound.
No kernel may reach another device: no remote copies, remote signals or barrier semaphores. Data moves between devices by JAX's collectives and lax.ppermute only.
A program may use at most 256 MiB of HBM per device.

```python
import jax
import jax.numpy as jnp
from jax import lax

D = 768
FF = 3072
HEADS = 12
HEAD_DIM = 64
BLOCK = 64
GLOBAL_BLOCKS = 2
RANDOM = 3
MAXDOC = 4096
SEGMENT = 4096
TOKENS = 32768
NBLOCKS = 512
DOCS = 12
N_BLK = 8


def doc_layout(key):
    groups = TOKENS // (2 * MAXDOC)
    middle_groups = groups - 1
    doc_blocks = MAXDOC // BLOCK
    fewest = doc_blocks // 2
    most = 5 * doc_blocks // 6
    layout_key = jax.random.fold_in(key, 11)
    key_first, key_second, key_forced, key_picks = jax.random.split(layout_key, 4)
    first_length = jax.random.randint(key_first, (middle_groups,), fewest, most + 1) * BLOCK
    second_length = jax.random.randint(key_second, (middle_groups,), fewest, most + 1) * BLOCK
    forced = jax.random.randint(key_forced, (), 0, middle_groups)
    chosen = jnp.arange(middle_groups) == forced
    first_length = jnp.where(chosen, MAXDOC, first_length)
    second_length = jnp.where(chosen, doc_blocks // 2 * BLOCK, second_length)
    third_length = 2 * MAXDOC - first_length - second_length
    middle_lengths = jnp.stack([first_length, second_length, third_length], axis=1).reshape(-1)
    opening = MAXDOC // 2 + BLOCK // 2
    closing_first = 3 * MAXDOC // 4
    closing_second = 2 * MAXDOC - opening - closing_first
    lengths = jnp.concatenate([jnp.full((1,), opening, dtype=jnp.int32), middle_lengths.astype(jnp.int32), jnp.array([closing_first, closing_second], dtype=jnp.int32)]).astype(jnp.int32)
    starts = (jnp.cumsum(lengths) - lengths).astype(jnp.int32)
    return (starts, lengths, key_picks)


def draw_doc_starts(key, part):
    return doc_layout(key)[0]


def draw_random_blocks(key, part):
    starts, lengths, key_picks = doc_layout(key)
    lead_tokens = jnp.arange(NBLOCKS, dtype=jnp.int32) * BLOCK
    before = starts[None, :] <= lead_tokens[:, None]
    doc_index = jnp.sum(before.astype(jnp.int32), axis=1) - 1
    owner_hot = jnp.arange(DOCS, dtype=jnp.int32)[None, :] == doc_index[:, None]
    doc_first = jnp.sum(jnp.where(owner_hot, starts[None, :], 0), axis=1)
    doc_length = jnp.sum(jnp.where(owner_hot, lengths[None, :], 0), axis=1)
    low_block = doc_first // BLOCK
    high_block = (doc_first + doc_length - 1) // BLOCK
    picks = jax.random.randint(key_picks, (NBLOCKS, RANDOM), low_block[:, None], high_block[:, None] + 1)
    return picks.astype(jnp.int32)


def spiked(values, key, source, target, blocks, factor):
    owner, partner = [(jnp.arange(values.shape[position]) // (values.shape[position] // blocks)).reshape([-1 if axis == position else 1 for axis in range(values.ndim)]) for position in (source, target)]
    chosen = jax.random.permutation(key, blocks)[partner]
    strong = (owner == chosen) | (owner == (partner + blocks // 2) % blocks)
    return jnp.where(strong, factor * values, values)


def levels(key, shape, cuts, smallest, high):
    factor_of = 1.0
    for dim, shards_of in cuts:
        steps = jax.random.uniform(jax.random.fold_in(jax.random.fold_in(key, 6), dim), (shards_of,), jnp.float32, smallest / len(cuts), high / len(cuts))
        factor_of = factor_of * jnp.repeat(jnp.exp(steps), shape[dim] // shards_of).reshape((-1,) + (1,) * (len(shape) - 1 - dim))
    return factor_of


def bell_draw(stream_key, extent, deviation, most, cuts=(), kind=jnp.bfloat16):
    entries = jax.random.normal(stream_key, extent, jnp.float32) * deviation
    if len(cuts) > 0:
        entries = levels(stream_key, extent, cuts, -0.22, 0.18) * entries
    return jnp.clip(entries, min=-most, max=most).astype(kind)


def gaussian_with(own_key, dims, scale, reach, shards, heavy, held_as=jnp.bfloat16):
    entries = scale * jax.random.normal(own_key, dims, jnp.float32)
    if shards:
        entries = entries * levels(own_key, dims, shards, -0.22, 0.18)
    return jnp.clip(spiked(entries, jax.random.fold_in(own_key, 3), *heavy), -reach, reach).astype(held_as)


def setup_inputs(seed: int = 0) -> dict:
    arg_keys = jax.random.split(jax.random.key(seed), 20)
    return {
        "tokens_in": bell_draw(arg_keys[0], (N_BLK, SEGMENT, D), 1.0, 6.0, ((0, 8), (1, 4))),
        "query_weight": bell_draw(arg_keys[1], (D, D), D ** -0.5, 0.21875, ((0, 32),), jnp.float32),
        "query_bias": bell_draw(arg_keys[2], (D,), 0.5, 3.0, ((0, 32),), jnp.float32),
        "key_weight": bell_draw(arg_keys[3], (D, D), D ** -0.5, 0.21875, ((0, 32),), jnp.float32),
        "value_weight": bell_draw(arg_keys[4], (D, D), D ** -0.5, 0.21875, ((0, 32),), jnp.float32),
        "value_bias": bell_draw(arg_keys[5], (D,), 0.5, 3.0, ((0, 32),), jnp.float32),
        "mixer_weight": bell_draw(arg_keys[6], (D, D), (D // 256) ** -0.5, 3.5, ((0, 32),), jnp.float32),
        "mixer_bias": bell_draw(arg_keys[7], (D,), 0.3, 2.0, ((0, 32),), jnp.float32),
        "first_gain": jnp.clip(1.0 + 0.1 * jax.random.normal(arg_keys[8], (D,), jnp.float32), 0.5, 1.5),
        "first_shift": bell_draw(arg_keys[9], (D,), 0.3, 2.0, ((0, 32),), jnp.float32),
        "expand_weight": bell_draw(arg_keys[10], (D, FF), D ** -0.5, 0.21875, ((0, 32),), jnp.float32),
        "expand_bias": bell_draw(arg_keys[11], (FF,), 0.5, 3.0, ((0, 32),), jnp.float32),
        "shrink_weight": bell_draw(arg_keys[12], (FF, D), FF ** -0.5, 0.109375, ((0, 32),), jnp.float32),
        "shrink_bias": bell_draw(arg_keys[13], (D,), 0.3, 2.0, ((0, 32),), jnp.float32),
        "second_gain": jnp.clip(1.0 + 0.1 * jax.random.normal(arg_keys[14], (D,), jnp.float32), 0.5, 1.5),
        "second_shift": bell_draw(arg_keys[15], (D,), 0.3, 2.0, ((0, 32),), jnp.float32),
        "doc_starts": draw_doc_starts(jax.random.fold_in(arg_keys[19], 71), 0),
        "random_blocks": draw_random_blocks(jax.random.fold_in(arg_keys[19], 71), 0),
        "cotangent": gaussian_with(arg_keys[18], (N_BLK, SEGMENT, D), 1.0, 6.0, ((0, 8), (1, 4)), (0, 2, 8, 2.0)),
    }


@jax.custom_vjp
def low(v):
    return lax.optimization_barrier(v.astype(jnp.bfloat16)).astype(jnp.float32)

@jax.custom_vjp
def low_back(v):
    return v

def low_keep(v):
    return (low(v), None)

def low_pass(kept, grad):
    return (grad,)

def back_keep(v):
    return (v, None)

def back_low(kept, grad):
    return (low(grad),)
low.defvjp(low_keep, low_pass)
low_back.defvjp(back_keep, back_low)
highest = lax.Precision.HIGHEST
layer_eps = 1e-12
masked_score = -1e+30

def token_docs(positions, starts):
    before = starts[None, :] <= positions[:, None]
    doc_index = lax.optimization_barrier(jnp.sum(before.astype(jnp.int32), axis=1)) - 1
    doc_first = lax.optimization_barrier(jnp.max(jnp.where(before, starts[None, :], 0), axis=1))
    return (doc_index.astype(jnp.int32), doc_first.astype(jnp.int32))

def block_lists(block_ids, random_picks, starts, total_blocks):
    lead_tokens = block_ids * BLOCK
    first_lead = token_docs(lead_tokens, starts)[1]
    first_tail = token_docs(lead_tokens + BLOCK - 1, starts)[1]
    columns = [block_ids - 1, block_ids, block_ids + 1]
    columns += [random_picks[:, pick] for pick in range(random_picks.shape[1])]
    for anchor in (first_lead, first_tail):
        columns += [anchor // BLOCK + offset for offset in range(GLOBAL_BLOCKS + 1)]
    candidate = jnp.clip(jnp.stack(columns, axis=1), 0, total_blocks - 1).astype(jnp.int32)
    repeats = [jnp.zeros(candidate.shape[:1], dtype=jnp.bool_)]
    for column in range(1, candidate.shape[1]):
        repeats.append(jnp.any(candidate[:, :column] == candidate[:, column:column + 1], axis=1))
    distinct = jnp.logical_not(jnp.stack(repeats, axis=1))
    nearby = jnp.logical_or(jnp.abs(candidate - block_ids[:, None]) <= 1, jnp.any(candidate[:, :, None] == random_picks[:, None, :], axis=2))
    return (candidate, distinct, nearby)

def allowed_mask(key_doc, candidate, distinct, nearby, query_doc, query_first):
    key_pos = candidate[..., None] * BLOCK + jnp.arange(BLOCK, dtype=jnp.int32)
    same_doc = key_doc[:, None] == query_doc[:, :, None, None]
    early_key = key_pos[:, None] - query_first[:, :, None, None] < GLOBAL_BLOCKS * BLOCK
    return same_doc & distinct[:, None, :, None] & (nearby[:, None, :, None] | early_key)

def norm_rows(values_in, gain_row, shift_row):
    row_mean = lax.optimization_barrier(jnp.mean(values_in, axis=-1, keepdims=True))
    centred = values_in - row_mean
    spread = lax.optimization_barrier(jnp.mean(centred * centred, axis=-1, keepdims=True))
    return centred * lax.rsqrt(spread + layer_eps) * gain_row + shift_row

def gelu_exact(values_in):
    return jax.nn.gelu(values_in, approximate=False)

def attention(queries, key_rows, value_rows, layout):
    doc_of, first_of, candidate, distinct, nearby = layout
    tile_count = NBLOCKS // 8
    key_blocks = key_rows.reshape(NBLOCKS, BLOCK, HEADS, HEAD_DIM)
    value_blocks = value_rows.reshape(NBLOCKS, BLOCK, HEADS, HEAD_DIM)
    doc_blocks = doc_of.reshape(NBLOCKS, BLOCK)

    def tile_work(key_blocks, value_blocks, piece):
        query_tile, query_doc, query_first, tile_cand, tile_distinct, tile_nearby = piece
        near_keys = key_blocks[tile_cand]
        near_values = value_blocks[tile_cand]
        raw_scores = jnp.einsum('bqhd,bckhd->bhqck', query_tile, near_keys, precision=highest)
        scores = low_back(raw_scores) * HEAD_DIM ** (-0.5)
        key_mask = allowed_mask(doc_blocks[tile_cand], tile_cand, tile_distinct, tile_nearby, query_doc, query_first)
        scores = jnp.where(key_mask[:, None], scores, masked_score)
        flat_scores = scores.reshape(scores.shape[0], HEADS, BLOCK, -1)
        soft_probs = jax.nn.softmax(flat_scores, axis=-1)
        flat_values = near_values.reshape(near_values.shape[0], -1, HEADS, HEAD_DIM)
        return jnp.einsum('bhqn,bnhd->bqhd', low(soft_probs), flat_values, precision=highest)
    checkpointed = jax.checkpoint(tile_work)

    def tile_step(piece):
        return checkpointed(key_blocks, value_blocks, piece)
    pieces = (queries.reshape(tile_count, 8, BLOCK, HEADS, HEAD_DIM), doc_of.reshape(tile_count, 8, BLOCK), first_of.reshape(tile_count, 8, BLOCK), candidate.reshape(tile_count, 8, -1), distinct.reshape(tile_count, 8, -1), nearby.reshape(tile_count, 8, -1))
    mixed_out = lax.map(tile_step, pieces)
    return mixed_out.reshape(TOKENS, D)

def forward(inputs, masters, layout):
    query_weight, query_bias, key_weight, value_weight, value_bias, mixer_weight, mixer_bias, first_gain, first_shift, expand_weight, expand_bias, shrink_weight, shrink_bias, second_gain, second_shift = [low(master) for master in masters]
    row_values = low(inputs)
    queries = low_back(low(jnp.dot(row_values, query_weight, precision=highest) + query_bias))
    key_rows = low_back(low(jnp.dot(row_values, key_weight, precision=highest)))
    value_rows = low_back(low(jnp.dot(row_values, value_weight, precision=highest) + value_bias))
    attended = low_back(low(attention(queries, key_rows, value_rows, layout)))
    branch = low_back(jnp.dot(attended, mixer_weight, precision=highest) + mixer_bias)
    middle = norm_rows(inputs + branch, first_gain, first_shift)
    pre_act = low_back(jnp.dot(low(middle), expand_weight, precision=highest) + expand_bias)
    active = low(gelu_exact(pre_act))
    ffn_out = low_back(jnp.dot(active, shrink_weight, precision=highest) + shrink_bias)
    return norm_rows(middle + ffn_out, second_gain, second_shift)

def reference(tokens_in, query_weight, query_bias, key_weight, value_weight, value_bias, mixer_weight, mixer_bias, first_gain, first_shift, expand_weight, expand_bias, shrink_weight, shrink_bias, second_gain, second_shift, doc_starts, random_blocks, cotangent):
    inputs = tokens_in.astype(jnp.float32).reshape(TOKENS, D)
    positions = jnp.arange(TOKENS, dtype=jnp.int32)
    doc_of, first_of = token_docs(positions, doc_starts)
    block_ids = jnp.arange(NBLOCKS, dtype=jnp.int32)
    candidate, distinct, nearby = block_lists(block_ids, random_blocks, doc_starts, NBLOCKS)
    layout = (doc_of, first_of, candidate, distinct, nearby)
    masters = (query_weight, query_bias, key_weight, value_weight, value_bias, mixer_weight, mixer_bias, first_gain, first_shift, expand_weight, expand_bias, shrink_weight, shrink_bias, second_gain, second_shift)

    def whole(inputs, masters):
        return forward(inputs, masters, layout)
    layer_out, pullback = jax.vjp(whole, inputs, masters)
    grad_inputs, grads = pullback(cotangent.astype(jnp.float32).reshape(TOKENS, D))
    return (layer_out.astype(jnp.bfloat16).reshape(N_BLK, SEGMENT, D), grad_inputs.reshape(N_BLK, SEGMENT, D), grads[0], grads[1], grads[2], grads[3], grads[4], grads[5], grads[6], grads[7], grads[8], grads[9], grads[10], grads[11], grads[12], grads[13], grads[14])
```

```python
import functools
import math

import jax
import jax.numpy as jnp
from jax import lax
from jax.experimental import pallas as pl
from jax.experimental.pallas import tpu as pltpu
from jax.sharding import PartitionSpec as P

HEADS = 12
HEAD_DIM = 64
BLOCK = 64
GLOBAL_BLOCKS = 2
MAXDOC = 4096
VMEM_BYTES = 60 * 2**20

layer_eps = 1e-12
masked_score = -1e30

def chunk_tile(rows, width):
    return lax.broadcasted_iota(jnp.int32, (rows, width), 1) // HEAD_DIM


def head_diag(tile, heads):
    owner = chunk_tile(BLOCK, heads * HEAD_DIM)
    return jnp.concatenate(
        [jnp.where(owner == head, tile, jnp.zeros_like(tile)) for head in range(heads)], axis=0
    )


def diag_rows(full, heads):
    owner = chunk_tile(BLOCK, heads * HEAD_DIM)
    picked = full[:BLOCK]
    for head in range(1, heads):
        picked = jnp.where(owner == head, full[head * BLOCK : (head + 1) * BLOCK], picked)
    return picked


def tile_bias(block, count, slots, place_ref, base_ref, kind_ref, first_ref, end_ref):
    first = first_ref[pl.ds(block, 1), :]
    end = end_ref[pl.ds(block, 1), :]
    key = lax.broadcasted_iota(jnp.int32, (BLOCK, 2 * BLOCK), 0)
    starts = []
    biases = []
    for slot in range(count):
        entry = block * slots + slot
        starts.append(pl.multiple_of(place_ref[entry] * BLOCK, BLOCK))
        base = base_ref[entry]
        kind = kind_ref[entry]
        high = jnp.where(kind == 2, end, first + GLOBAL_BLOCKS * BLOCK)
        high = jnp.where(kind == 0, -1, high - base)
        allowed = (key >= first - base) & (key < high)
        biases.append(jnp.where(allowed, 0.0, masked_score))
    return starts, jnp.concatenate(biases, axis=0)


NT = (((1,), (1,)), ((), ()))
NN = (((1,), (0,)), ((), ()))
TN = (((0,), (0,)), ((), ()))


def soft_columns(keys, query_diag, bias, heads):
    scores = lax.dot_general(keys, query_diag, NT, preferred_element_type=jnp.float32)
    scores = scores + jnp.concatenate([bias] * (heads // 2), axis=1)
    top = jnp.max(scores, axis=0, keepdims=True)
    raised = jnp.exp(scores - top)
    total = jnp.sum(raised, axis=0, keepdims=True)
    return raised * (1.0 / total)


def load_pool(chunks, pool_ref, sems):
    rows = chunks[0].shape[0]
    copies = [
        pltpu.make_async_copy(chunk, pool_ref.at[pl.ds(n * rows, rows)], sems.at[n])
        for n, chunk in enumerate(chunks)
    ]
    for copy in copies:
        copy.start()
    return copies


def attend_kernel(sizes, *refs):
    blocks, slots, few, groups, width = sizes
    place_ref, base_ref, kind_ref, count_ref, first_ref, end_ref, query_ref = refs[:7]
    chunks = refs[7:-3]
    out_ref, pool_ref, sems = refs[-3:]
    for copy in load_pool(chunks, pool_ref, sems):
        copy.wait()

    def work(block, count):
        starts, bias = tile_bias(
            block, count, slots, place_ref, base_ref, kind_ref, first_ref, end_ref
        )
        here = pl.ds(pl.multiple_of(block * BLOCK, BLOCK), BLOCK)
        for low, heads in groups:
            span = heads * HEAD_DIM
            keys = jnp.concatenate(
                [pool_ref[pl.ds(start, BLOCK), low : low + span] for start in starts], axis=0
            )
            values = jnp.concatenate(
                [
                    pool_ref[pl.ds(start, BLOCK), width + low : width + low + span]
                    for start in starts
                ],
                axis=0,
            )
            query_diag = head_diag(query_ref[here, low : low + span], heads)
            probs = soft_columns(keys, query_diag, bias, heads).astype(jnp.bfloat16)
            mixed = lax.dot_general(probs, values, TN, preferred_element_type=jnp.float32)
            out_ref[here, low : low + span] = diag_rows(mixed, heads).astype(jnp.bfloat16)

    def step(block, carry):
        short = count_ref[block] <= few

        @pl.when(short)
        def _():
            work(block, few)

        @pl.when(jnp.logical_not(short))
        def _():
            work(block, slots)

        return carry

    lax.fori_loop(0, blocks, step, 0)


def attend_back_kernel(sizes, *refs):
    blocks, slots, few, groups, width, parts = sizes
    place_ref, base_ref, kind_ref, count_ref, first_ref, end_ref, query_ref, grad_ref = refs[:8]
    chunks = refs[8 : 8 + parts]
    query_grad_ref = refs[8 + parts]
    outs = refs[9 + parts : 9 + 2 * parts]
    pool_ref, total_ref, sems = refs[9 + 2 * parts :]
    copies = load_pool(chunks, pool_ref, sems)
    rows = chunks[0].shape[0]
    strip = 128

    def clear(n, carry):
        at = pl.ds(pl.multiple_of(n * strip, strip), strip)
        total_ref[at, :] = jnp.zeros((strip, 2 * width), jnp.float32)
        return carry

    lax.fori_loop(0, parts * rows // strip, clear, 0)
    for copy in copies:
        copy.wait()

    def work(block, count):
        starts, bias = tile_bias(
            block, count, slots, place_ref, base_ref, kind_ref, first_ref, end_ref
        )
        here = pl.ds(pl.multiple_of(block * BLOCK, BLOCK), BLOCK)
        for low, heads in groups:
            span = heads * HEAD_DIM
            keys = jnp.concatenate(
                [pool_ref[pl.ds(start, BLOCK), low : low + span] for start in starts], axis=0
            )
            values = jnp.concatenate(
                [
                    pool_ref[pl.ds(start, BLOCK), width + low : width + low + span]
                    for start in starts
                ],
                axis=0,
            )
            query_diag = head_diag(query_ref[here, low : low + span], heads)
            grad_diag = head_diag(grad_ref[here, low : low + span], heads)
            probs = soft_columns(keys, query_diag, bias, heads)
            grad_probs = lax.dot_general(values, grad_diag, NT, preferred_element_type=jnp.float32)
            inner = jnp.sum(probs * grad_probs, axis=0, keepdims=True)
            grad_scores = (probs * (grad_probs - inner)).astype(jnp.bfloat16)
            grad_values = lax.dot_general(
                probs.astype(jnp.bfloat16), grad_diag, NN, preferred_element_type=jnp.float32
            )
            grad_keys = lax.dot_general(
                grad_scores, query_diag, NN, preferred_element_type=jnp.float32
            )
            grad_query = lax.dot_general(grad_scores, keys, TN, preferred_element_type=jnp.float32)
            query_grad_ref[here, low : low + span] = (
                diag_rows(grad_query, heads) * HEAD_DIM**-0.5
            ).astype(jnp.bfloat16)
            for slot, start in enumerate(starts):
                lines = slice(slot * BLOCK, (slot + 1) * BLOCK)
                total_ref[pl.ds(start, BLOCK), low : low + span] += grad_keys[lines]
                total_ref[pl.ds(start, BLOCK), width + low : width + low + span] += grad_values[
                    lines
                ]

    def step(block, carry):
        short = count_ref[block] <= few

        @pl.when(short)
        def _():
            work(block, few)

        @pl.when(jnp.logical_not(short))
        def _():
            work(block, slots)

        return carry

    lax.fori_loop(0, blocks, step, 0)

    def lower(n, carry):
        at = pl.ds(pl.multiple_of(n * strip, strip), strip)
        pool_ref[at, :] = total_ref[at, :].astype(jnp.bfloat16)
        return carry

    sends = []
    for n, out in enumerate(outs):
        lax.fori_loop(n * rows // strip, (n + 1) * rows // strip, lower, 0)
        send = pltpu.make_async_copy(pool_ref.at[pl.ds(n * rows, rows)], out, sems.at[n])
        send.start()
        sends.append(send)
    for send in sends:
        send.wait()


def attend(lists, query_rows, chunks, groups, slots, few):
    tokens, width = query_rows.shape
    rows = chunks[0].shape[0]
    parts = len(chunks)
    blocks = tokens // BLOCK
    smem = pl.BlockSpec(memory_space=pltpu.SMEM)
    vmem = pl.BlockSpec(memory_space=pltpu.VMEM)
    hbm = pl.BlockSpec(memory_space=pl.ANY)
    keys = few * BLOCK
    return pl.pallas_call(
        functools.partial(attend_kernel, (blocks, slots, few, groups, width)),
        out_shape=jax.ShapeDtypeStruct((tokens, width), jnp.bfloat16),
        in_specs=[smem] * 4 + [vmem] * 3 + [hbm] * parts,
        out_specs=vmem,
        scratch_shapes=[
            pltpu.VMEM((parts * rows, 2 * width), jnp.bfloat16),
            pltpu.SemaphoreType.DMA((parts,)),
        ],
        compiler_params=pltpu.CompilerParams(vmem_limit_bytes=VMEM_BYTES),
        cost_estimate=pl.CostEstimate(
            flops=16 * tokens * keys * width,
            bytes_accessed=4 * parts * rows * width,
            transcendentals=tokens * keys * width // HEAD_DIM,
        ),
        name="attend",
    )(*lists, query_rows, *chunks)


def attend_back(lists, query_rows, grad_rows, chunks, groups, slots, few):
    tokens, width = query_rows.shape
    rows = chunks[0].shape[0]
    parts = len(chunks)
    blocks = tokens // BLOCK
    smem = pl.BlockSpec(memory_space=pltpu.SMEM)
    vmem = pl.BlockSpec(memory_space=pltpu.VMEM)
    hbm = pl.BlockSpec(memory_space=pl.ANY)
    keys = few * BLOCK
    return pl.pallas_call(
        functools.partial(attend_back_kernel, (blocks, slots, few, groups, width, parts)),
        out_shape=[jax.ShapeDtypeStruct((tokens, width), jnp.bfloat16)]
        + [jax.ShapeDtypeStruct((rows, 2 * width), jnp.bfloat16)] * parts,
        in_specs=[smem] * 4 + [vmem] * 4 + [hbm] * parts,
        out_specs=[vmem] + [hbm] * parts,
        scratch_shapes=[
            pltpu.VMEM((parts * rows, 2 * width), jnp.bfloat16),
            pltpu.VMEM((parts * rows, 2 * width), jnp.float32),
            pltpu.SemaphoreType.DMA((parts,)),
        ],
        compiler_params=pltpu.CompilerParams(vmem_limit_bytes=VMEM_BYTES),
        cost_estimate=pl.CostEstimate(
            flops=40 * tokens * keys * width,
            bytes_accessed=8 * parts * rows * width,
            transcendentals=tokens * keys * width // HEAD_DIM,
        ),
        name="attend_back",
    )(*lists, query_rows, grad_rows, *chunks)


def token_docs(positions, starts):
    before = starts[None, :] <= positions[:, None]
    return jnp.max(jnp.where(before, starts[None, :], 0), axis=1)


def token_ends(positions, starts, tokens):
    after = starts[None, :] > positions[:, None]
    return jnp.min(jnp.where(after, starts[None, :], tokens), axis=1)


def block_lists(block_ids, random_picks, starts, total_blocks):
    lead_tokens = block_ids * BLOCK
    first_lead = token_docs(lead_tokens, starts)
    first_tail = token_docs(lead_tokens + BLOCK - 1, starts)
    end_tail = token_ends(lead_tokens + BLOCK - 1, starts, total_blocks * BLOCK)
    columns = [block_ids - 1, block_ids, block_ids + 1]
    columns += [random_picks[:, pick] for pick in range(random_picks.shape[1])]
    for anchor in (first_lead, first_tail):
        columns += [anchor // BLOCK + offset for offset in range(GLOBAL_BLOCKS + 1)]
    candidate = jnp.clip(jnp.stack(columns, axis=1), 0, total_blocks - 1)
    repeats = [jnp.zeros(candidate.shape[:1], dtype=jnp.bool_)]
    for column in range(1, candidate.shape[1]):
        repeats.append(jnp.any(candidate[:, :column] == candidate[:, column : column + 1], axis=1))
    distinct = jnp.logical_not(jnp.stack(repeats, axis=1))
    nearby = jnp.logical_or(
        jnp.abs(candidate - block_ids[:, None]) <= 1,
        jnp.any(candidate[:, :, None] == random_picks[:, None, :], axis=2),
    )
    lead = candidate * BLOCK
    reached = (lead + BLOCK > first_lead[:, None]) & (lead < end_tail[:, None])
    reached &= nearby | (lead < first_tail[:, None] + GLOBAL_BLOCKS * BLOCK)
    return candidate, distinct & reached, nearby


def norm_rows(values_in, gain_row, shift_row):
    row_mean = jnp.mean(values_in, axis=-1, keepdims=True)
    centred = values_in - row_mean
    spread = jnp.mean(centred * centred, axis=-1, keepdims=True)
    return centred * lax.rsqrt(spread + layer_eps) * gain_row + shift_row


def gelu_exact(values_in):
    return jax.nn.gelu(values_in, approximate=False)


def pick(flag, first, second):
    return jnp.where(flag == 0, first, second)


def split_low(wide, width):
    high = lax.reduce_precision(wide, 8, 7)
    parts = [high.astype(jnp.bfloat16), (wide - high).astype(jnp.bfloat16)]
    pad = width - 2 * wide.shape[-1]
    parts.append(jnp.zeros(wide.shape[:-1] + (pad,), jnp.bfloat16))
    return jnp.concatenate(parts, axis=-1)


def join_low(packed, count):
    wide = packed.astype(jnp.float32)
    return wide[..., :count] + wide[..., count : 2 * count]


def body(
    tokens_in,
    query_weight,
    query_bias,
    key_weight,
    value_weight,
    value_bias,
    mixer_weight,
    mixer_bias,
    first_gain,
    first_shift,
    expand_weight,
    expand_bias,
    shrink_weight,
    shrink_bias,
    second_gain,
    second_shift,
    doc_starts,
    random_blocks,
    cotangent,
):
    f32 = jnp.float32
    bf16 = jnp.bfloat16
    axes = ("head", "blk")
    head_count = lax.axis_size("head")
    cycle_size = lax.axis_size("blk")
    devices = head_count * cycle_size
    head_index = lax.axis_index("head")
    cycle_index = lax.axis_index("blk")
    side = head_index // 2
    core = head_index % 2
    local_rows = tokens_in.shape[1]
    model_width = tokens_in.shape[2]
    half_width = model_width // 2
    hidden = expand_weight.shape[1]
    fold = hidden // model_width
    own_rows = query_weight.shape[0]
    part_blocks = local_rows // BLOCK
    half_blocks = 2 * part_blocks
    total_blocks = part_blocks * devices
    slots = 3 + random_blocks.shape[1] + 2 * (GLOBAL_BLOCKS + 1)
    few = slots - GLOBAL_BLOCKS - 1
    groups = ((0, 4), (4 * HEAD_DIM, 2))

    def flat(head, cycle):
        return head * cycle_size + cycle

    everywhere = [(h, b) for h in range(head_count) for b in range(cycle_size)]
    over_side = [(flat(h, b), flat(h ^ 2, b)) for h, b in everywhere]
    over_core = [(flat(h, b), flat(h ^ 1, b)) for h, b in everywhere]
    inward = [
        (flat(h, b), flat(h, b + (1 if h >= 2 else -1)))
        for h, b in everywhere
        if 0 <= b + (1 if h >= 2 else -1) < cycle_size
    ]
    outward = [
        (flat(h, b), flat(h, b + (-1 if h >= 2 else 1)))
        for h, b in everywhere
        if 0 <= b + (-1 if h >= 2 else 1) < cycle_size
    ]

    def send(array, pairs):
        return lax.ppermute(array, axes, pairs)

    def send_back(array, pairs):
        return lax.ppermute(array, axes, [(b, a) for a, b in pairs])

    inputs = tokens_in[0]
    beside = send(inputs, over_side)
    near = send(inputs, inward)
    passed = send(near, over_side)
    far = send(inputs, outward)
    held = [inputs, beside, near, passed, far]

    low_query = query_weight.astype(bf16)
    low_key = key_weight.astype(bf16)
    low_value = value_weight.astype(bf16)
    vectors = [
        query_bias,
        value_bias,
        mixer_bias,
        first_gain,
        first_shift,
        shrink_bias,
        second_gain,
        second_shift,
    ]
    lines = [vector[:, None] for vector in vectors] + [expand_bias.reshape(own_rows, fold)]
    line_count = len(vectors) + fold
    line_width = 128
    lines.append(jnp.zeros((own_rows, line_width - line_count), f32))
    shard = jnp.concatenate(
        [
            low_key[:, :half_width],
            low_value[:, :half_width],
            low_query[:, :half_width],
            low_key[:, half_width:],
            low_value[:, half_width:],
            low_query[:, half_width:],
            jnp.concatenate(lines, axis=1).astype(bf16),
        ],
        axis=1,
    )
    trio = 3 * half_width
    spread = jnp.broadcast_to(shard[None], (cycle_size,) + shard.shape)
    column = lax.all_to_all(spread, "blk", split_axis=0, concat_axis=0, tiled=True)
    column = column.reshape(cycle_size * own_rows, -1)
    column_beside = send(column, over_side)
    pair = pick(side, jnp.stack([column, column_beside]), jnp.stack([column_beside, column]))
    wanted = jnp.concatenate(
        [pick(core, pair[..., :trio], pair[..., trio : 2 * trio]), pair[..., 2 * trio :]], axis=2
    )
    unwanted = jnp.concatenate(
        [pick(core, pair[..., trio : 2 * trio], pair[..., :trio]), pair[..., 2 * trio :]], axis=2
    )
    given = send(unwanted, over_core)
    table = pick(core, jnp.stack([wanted, given], axis=1), jnp.stack([given, wanted], axis=1))
    table = table.reshape(model_width, trio + line_width)
    pair_matrix = table[:, :model_width]
    query_matrix = table[:, model_width:trio]
    vector_rows = table[:, trio : trio + line_count].astype(f32).T
    query_offset = pick(core, vector_rows[0, :half_width], vector_rows[0, half_width:])
    value_offset = pick(core, vector_rows[1, :half_width], vector_rows[1, half_width:])
    mixer_offset, first_scale, first_level, shrink_offset, second_scale, second_level = [
        vector_rows[n] for n in range(2, len(vectors))
    ]
    expand_offset = table[:, trio + len(vectors) : trio + line_count].astype(f32).reshape(hidden)
    pair_offset = jnp.concatenate([jnp.zeros((half_width,), f32), value_offset])

    bundle = jnp.concatenate(
        [
            expand_weight.astype(bf16).reshape(own_rows * fold, model_width),
            shrink_weight.astype(bf16),
            mixer_weight.astype(bf16),
        ],
        axis=0,
    )
    wide_rows = own_rows * fold
    bundles = lax.all_gather(bundle, axes, axis=0, tiled=True).reshape(
        devices, bundle.shape[0], model_width
    )
    expand_matrix = bundles[:, :wide_rows].reshape(model_width, hidden)
    shrink_matrix = bundles[:, wide_rows : 2 * wide_rows].reshape(hidden, model_width)
    mixer_matrix = bundles[:, 2 * wide_rows :].reshape(model_width, model_width)

    half_index = 2 * cycle_index + side
    block_of = jnp.arange(half_blocks, dtype=jnp.int32)
    part_of = jnp.where(block_of < part_blocks, core, 1 - core)
    block_ids = half_index * half_blocks + part_of * part_blocks + block_of % part_blocks
    picks = jnp.concatenate(
        [
            lax.dynamic_slice_in_dim(random_blocks, head_index * part_blocks, part_blocks),
            lax.dynamic_slice_in_dim(random_blocks, (head_index ^ 1) * part_blocks, part_blocks),
        ],
        axis=0,
    )
    candidate, useful, nearby = block_lists(block_ids, picks, doc_starts, total_blocks)
    apart = candidate // half_blocks - half_index
    reach = jnp.abs(apart)
    useful = useful & (reach <= 2)
    slot_of = jnp.where((apart > 0) == (side == 0), reach, reach + 2)
    slot_of = jnp.where(apart == 0, 0, slot_of)
    part_at = (candidate // part_blocks) % 2 != core
    place = (2 * slot_of + part_at.astype(jnp.int32)) * part_blocks + candidate % part_blocks
    earlier = jnp.arange(slots)[None, :] < jnp.arange(slots)[:, None]
    rank = jnp.sum((useful[:, None, :] & earlier[None]).astype(jnp.int32), axis=2)
    seat = useful[:, :, None] & (rank[:, :, None] == jnp.arange(slots)[None, None, :])

    def seated(values):
        return jnp.sum(jnp.where(seat, values[:, :, None], 0), axis=1).reshape(-1)

    query_positions = (
        block_ids[:, None] * BLOCK + jnp.arange(BLOCK, dtype=jnp.int32)[None, :]
    ).reshape(-1)
    query_first = token_docs(query_positions, doc_starts).reshape(half_blocks, BLOCK)
    query_end = token_ends(query_positions, doc_starts, total_blocks * BLOCK).reshape(
        half_blocks, BLOCK
    )
    lists = (
        seated(place),
        seated(candidate * BLOCK),
        seated(1 + nearby.astype(jnp.int32)),
        jnp.sum(useful.astype(jnp.int32), axis=1),
        jnp.concatenate([query_first, query_first], axis=1),
        jnp.concatenate([query_end, query_end], axis=1),
    )

    def project(rows, matrix, offset):
        return (jnp.dot(rows, matrix, preferred_element_type=f32) + offset).astype(bf16)

    rows_in = []
    for array in held:
        rows_in += [array, send(array, over_core)]
    query_rows = jnp.concatenate(
        [project(rows, query_matrix, query_offset) for rows in rows_in[:2]], axis=0
    ) * jnp.asarray(HEAD_DIM**-0.5, bf16)
    chunks = [project(rows, pair_matrix, pair_offset) for rows in rows_in]
    mixed = attend(lists, query_rows, chunks, groups, slots, few)
    mixed_given = send(mixed[local_rows:], over_core)
    mixed_kept = mixed[:local_rows]
    attended = pick(
        core,
        jnp.concatenate([mixed_kept, mixed_given], axis=1),
        jnp.concatenate([mixed_given, mixed_kept], axis=1),
    )

    first_sum = (
        inputs.astype(f32)
        + jnp.dot(attended, mixer_matrix, preferred_element_type=f32)
        + mixer_offset
    )
    middle, first_back = jax.vjp(norm_rows, first_sum, first_scale, first_level)
    middle_low = middle.astype(bf16)
    pre_act = jnp.dot(middle_low, expand_matrix, preferred_element_type=f32) + expand_offset
    active_wide, gelu_back = jax.vjp(gelu_exact, pre_act)
    active = active_wide.astype(bf16)
    second_sum = (
        middle + jnp.dot(active, shrink_matrix, preferred_element_type=f32) + shrink_offset
    )
    layer_out, second_back = jax.vjp(norm_rows, second_sum, second_scale, second_level)
    grad_second, second_scale_grad, second_level_grad = second_back(cotangent[0].astype(f32))
    grad_ffn = grad_second.astype(bf16)
    shrink_grad = jnp.einsum("tf,td->fd", active, grad_ffn, preferred_element_type=f32)
    shrink_bias_grad = jnp.sum(grad_ffn.astype(f32), axis=0)
    grad_active = jnp.einsum("td,fd->tf", grad_ffn, shrink_matrix, preferred_element_type=f32)
    grad_pre = gelu_back(grad_active)[0].astype(bf16)
    expand_grad = jnp.einsum("td,tf->df", middle_low, grad_pre, preferred_element_type=f32)
    expand_bias_grad = jnp.sum(grad_pre.astype(f32), axis=0)
    grad_middle = grad_second + jnp.einsum(
        "tf,df->td", grad_pre, expand_matrix, preferred_element_type=f32
    )
    grad_first, first_scale_grad, first_level_grad = first_back(grad_middle)
    grad_branch = grad_first.astype(bf16)
    mixer_grad = jnp.einsum("td,te->de", attended, grad_branch, preferred_element_type=f32)
    mixer_bias_grad = jnp.sum(grad_branch.astype(f32), axis=0)
    grad_attended = jnp.einsum(
        "te,de->td", grad_branch, mixer_matrix, preferred_element_type=f32
    ).astype(bf16)
    grad_kept = pick(core, grad_attended[:, :half_width], grad_attended[:, half_width:])
    grad_given = send(
        pick(core, grad_attended[:, half_width:], grad_attended[:, :half_width]), over_core
    )

    grad_bundle = jnp.concatenate(
        [
            expand_grad.astype(bf16).reshape(devices, wide_rows, model_width),
            shrink_grad.astype(bf16).reshape(devices, wide_rows, model_width),
            mixer_grad.astype(bf16).reshape(devices, own_rows, model_width),
        ],
        axis=1,
    ).reshape(-1, model_width)
    own_bundle = lax.psum_scatter(grad_bundle, axes, scatter_dimension=0, tiled=True).astype(f32)

    query_grad_rows, *pair_grads = attend_back(
        lists, query_rows, jnp.concatenate([grad_kept, grad_given], axis=0), chunks, groups, slots, few
    )
    query_grads = [query_grad_rows[:local_rows], query_grad_rows[local_rows:]]

    def back(grad, matrix):
        return jnp.einsum("te,de->td", grad, matrix, preferred_element_type=f32)

    partial = [back(grad, pair_matrix) for grad in pair_grads]
    partial[0] = partial[0] + back(query_grads[0], query_matrix)
    partial[1] = partial[1] + back(query_grads[1], query_matrix)
    totals = []
    for n in range(len(held)):
        totals.append(partial[2 * n] + send(partial[2 * n + 1].astype(bf16), over_core).astype(f32))
    own_total, beside_total, near_total, passed_total, far_total = totals
    near_total = near_total + send(passed_total.astype(bf16), over_side).astype(f32)
    input_grad = (
        grad_first
        + own_total
        + send(beside_total.astype(bf16), over_side).astype(f32)
        + send_back(far_total.astype(bf16), outward).astype(f32)
        + send_back(near_total.astype(bf16), inward).astype(f32)
    )

    pair_weight_grad = sum(
        jnp.einsum("td,te->de", rows, grad, preferred_element_type=f32)
        for rows, grad in zip(rows_in, pair_grads)
    )
    query_weight_grad = sum(
        jnp.einsum("td,te->de", rows, grad, preferred_element_type=f32)
        for rows, grad in zip(rows_in, query_grads)
    )
    value_bias_grad = sum(jnp.sum(grad[:, half_width:].astype(f32), axis=0) for grad in pair_grads)
    query_bias_grad = sum(jnp.sum(grad.astype(f32), axis=0) for grad in query_grads)

    def placed(half_row):
        nothing = jnp.zeros_like(half_row)
        return pick(
            core,
            jnp.concatenate([half_row, nothing]),
            jnp.concatenate([nothing, half_row]),
        )

    line_rows = jnp.stack(
        [
            placed(query_bias_grad),
            placed(value_bias_grad),
            mixer_bias_grad,
            first_scale_grad,
            first_level_grad,
            shrink_bias_grad,
            second_scale_grad,
            second_level_grad,
        ]
    )
    line_grads = jnp.concatenate([line_rows.T, expand_bias_grad.reshape(model_width, fold)], axis=1)
    stage = (2, 2, cycle_size * own_rows)
    table_grad = jnp.concatenate([pair_weight_grad, query_weight_grad], axis=1).reshape(
        stage + (trio,)
    )
    line_grads = line_grads.reshape(stage + (line_count,))
    kept = pick(core, table_grad[:, 0], table_grad[:, 1])
    kept_lines = pick(core, line_grads[:, 0], line_grads[:, 1])
    leaving = jnp.concatenate(
        [
            pick(core, table_grad[:, 1], table_grad[:, 0]).astype(bf16),
            split_low(pick(core, line_grads[:, 1], line_grads[:, 0]), line_width),
        ],
        axis=2,
    )
    arrived = send(leaving, over_core)
    brought = arrived[..., :trio].astype(f32)
    table_sum = pick(
        core,
        jnp.concatenate([kept, brought], axis=2),
        jnp.concatenate([brought, kept], axis=2),
    )
    line_sum = kept_lines + join_low(arrived[..., trio:], line_count)
    leaving = jnp.concatenate(
        [
            pick(side, table_sum[1], table_sum[0]).astype(bf16),
            split_low(pick(side, line_sum[1], line_sum[0]), line_width),
        ],
        axis=1,
    )
    arrived = send(leaving, over_side)
    table_sum = pick(side, table_sum[0], table_sum[1]) + arrived[:, : 2 * trio].astype(f32)
    line_sum = pick(side, line_sum[0], line_sum[1]) + join_low(arrived[:, 2 * trio :], line_count)
    leaving = jnp.concatenate([table_sum.astype(bf16), split_low(line_sum, line_width)], axis=1)
    arrived = lax.all_to_all(
        leaving.reshape(cycle_size, own_rows, -1), "blk", split_axis=0, concat_axis=0, tiled=True
    )
    table_own = jnp.sum(arrived[..., : 2 * trio].astype(f32), axis=0)
    line_own = jnp.sum(join_low(arrived[..., 2 * trio :], line_count), axis=0)

    def columns_of(which):
        low = which * half_width
        return jnp.concatenate(
            [table_own[:, low : low + half_width], table_own[:, trio + low : trio + low + half_width]],
            axis=1,
        )

    return (
        layer_out.astype(bf16)[None],
        input_grad[None],
        columns_of(2),
        line_own[:, 0],
        columns_of(0),
        columns_of(1),
        line_own[:, 1],
        own_bundle[2 * wide_rows :],
        line_own[:, 2],
        line_own[:, 3],
        line_own[:, 4],
        own_bundle[:wide_rows].reshape(own_rows, hidden),
        line_own[:, len(vectors) :].reshape(-1),
        own_bundle[wide_rows : 2 * wide_rows],
        line_own[:, 5],
        line_own[:, 6],
        line_own[:, 7],
    )


def solution(mesh):
    in_specs = (
        P("blk", "head", None),
        P(("head", "blk"), None),
        P(("head", "blk")),
        P(("head", "blk"), None),
        P(("head", "blk"), None),
        P(("head", "blk")),
        P(("head", "blk"), None),
        P(("head", "blk")),
        P(("head", "blk")),
        P(("head", "blk")),
        P(("head", "blk"), None),
        P(("head", "blk")),
        P(("head", "blk"), None),
        P(("head", "blk")),
        P(("head", "blk")),
        P(("head", "blk")),
        P(),
        P("blk", None),
        P("blk", "head", None),
    )
    out_specs = (
        P("blk", "head", None),
        P("blk", "head", None),
        P(("head", "blk"), None),
        P(("head", "blk")),
        P(("head", "blk"), None),
        P(("head", "blk"), None),
        P(("head", "blk")),
        P(("head", "blk"), None),
        P(("head", "blk")),
        P(("head", "blk")),
        P(("head", "blk")),
        P(("head", "blk"), None),
        P(("head", "blk")),
        P(("head", "blk"), None),
        P(("head", "blk")),
        P(("head", "blk")),
        P(("head", "blk")),
    )
    return jax.shard_map(body, mesh=mesh, in_specs=in_specs, out_specs=out_specs, check_vma=False)
```

```python
import functools
import math

import jax
import jax.numpy as jnp
from jax import lax
from jax.experimental import pallas as pl
from jax.experimental.pallas import tpu as pltpu
from jax.sharding import PartitionSpec as P

HEADS = 12
HEAD_DIM = 64
BLOCK = 64
GLOBAL_BLOCKS = 2
MAXDOC = 4096
VMEM_BYTES = 60 * 2**20

layer_eps = 1e-12
masked_score = -1e30

def pack_kernel(sizes, *refs):
    half, per_row, gap = sizes
    key_ref, value_ref, query_ref = refs[:3]
    vectors = refs[3:-1]
    out_ref = refs[-1]
    rows, total = out_ref.shape
    bf16 = jnp.bfloat16
    for n, source in enumerate((key_ref, value_ref, query_ref)):
        for core in range(2):
            at = (3 * core + n) * half
            out_ref[:, at : at + half] = source[:, core * half : (core + 1) * half].astype(bf16)
    line = lax.broadcasted_iota(jnp.int32, (rows, 128), 0)
    block = jnp.zeros((rows, 128), jnp.float32)
    for n, vector in enumerate(vectors):
        row = vector[...]
        low = n % per_row * gap
        pieces = [row, jnp.zeros((1, 128 - low - row.shape[1]), jnp.float32)]
        if low:
            pieces = [jnp.zeros((1, low), jnp.float32)] + pieces
        block = jnp.where(line == n // per_row, block + jnp.concatenate(pieces, axis=1), block)
    out_ref[:, 6 * half :] = block.astype(bf16)


def pack(key_weight, value_weight, query_weight, vectors, per_row, gap):
    rows, width = key_weight.shape
    vmem = pl.BlockSpec(memory_space=pltpu.VMEM)
    return pl.pallas_call(
        functools.partial(pack_kernel, (width // 2, per_row, gap)),
        out_shape=jax.ShapeDtypeStruct((rows, 3 * width + 128), jnp.bfloat16),
        in_specs=[vmem] * (3 + len(vectors)),
        out_specs=vmem,
        name="pack",
    )(key_weight, value_weight, query_weight, *[vector[None] for vector in vectors])


def list_kernel(sizes, spot_ref, starts_ref, picks_ref, *outs):
    place_ref, base_ref, kind_ref, count_ref, first_ref, end_ref = outs
    part_blocks, half_blocks, total_blocks, slots, random = sizes
    bits = BLOCK.bit_length() - 1
    part_bits = part_blocks.bit_length() - 1
    half_bits = half_blocks.bit_length() - 1
    lanes = 2 * BLOCK
    side, core, half_index = [spot_ref[n] for n in range(3)]
    docs = [starts_ref[n] for n in range(starts_ref.shape[0])]
    int32 = jnp.int32

    def block_of(n):
        part = jnp.where(n < part_blocks, core, 1 - core)
        return half_index * half_blocks + part * part_blocks + (n & (part_blocks - 1))

    def first_of(position):
        first = jnp.zeros(position.shape, int32)
        for start in docs:
            first = jnp.where(position >= start, start, first)
        return first

    def end_of(position):
        end = jnp.full(position.shape, total_blocks * BLOCK, int32)
        for start in docs[::-1]:
            end = jnp.where(position < start, start, end)
        return end

    rows = lax.broadcasted_iota(int32, (half_blocks, lanes), 0)
    columns = lax.broadcasted_iota(int32, (half_blocks, lanes), 1)
    positions = block_of(rows) * BLOCK + (columns & (BLOCK - 1))
    first_ref[...] = first_of(positions)
    end_ref[...] = end_of(positions)

    block = block_of(lax.broadcasted_iota(int32, (1, lanes), 1))
    lead = block * BLOCK
    first_lead = first_of(lead)
    first_tail = first_of(lead + BLOCK - 1)
    end_tail = end_of(lead + BLOCK - 1)
    picks = [picks_ref[pl.ds(n, 1), :] for n in range(random)]
    candidates = [block - 1, block, block + 1] + picks
    for anchor in (first_lead, first_tail):
        candidates += [(anchor >> bits) + offset for offset in range(GLOBAL_BLOCKS + 1)]
    candidates = [jnp.clip(candidate, 0, total_blocks - 1) for candidate in candidates]
    seated = [[jnp.zeros((1, lanes), int32)] * 3 for _ in range(slots)]
    rank = jnp.zeros((1, lanes), int32)
    for n, candidate in enumerate(candidates):
        useful = candidate >= 0
        for earlier in candidates[:n]:
            useful = useful & (candidate != earlier)
        nearby = jnp.abs(candidate - block) <= 1
        for chosen in picks:
            nearby = nearby | (candidate == chosen)
        base = candidate * BLOCK
        useful = useful & (base + BLOCK > first_lead) & (base < end_tail)
        useful = useful & (nearby | (base < first_tail + GLOBAL_BLOCKS * BLOCK))
        apart = (candidate >> half_bits) - half_index
        reach = jnp.abs(apart)
        useful = useful & (reach <= 2)
        later = (apart > 0).astype(int32)
        slot = jnp.where(later == 1 - side, reach, reach + 2)
        slot = jnp.where(reach == 0, 0, slot)
        part = ((candidate >> part_bits) & 1) ^ core
        place = (2 * slot + part) * part_blocks + (candidate & (part_blocks - 1))
        values = (place, base, 1 + nearby.astype(int32))
        for seat in range(n + 1):
            here = useful & (rank == seat)
            seated[seat] = [jnp.where(here, new, old) for new, old in zip(values, seated[seat])]
        rank = rank + useful.astype(int32)
    for seat in range(slots):
        for out, value in zip((place_ref, base_ref, kind_ref), seated[seat]):
            out[pl.ds(seat, 1), :] = value
    count_ref[...] = rank


def key_lists(spot, doc_starts, picks, part_blocks, total_blocks, slots, random):
    lanes = 2 * BLOCK
    half_blocks = 2 * part_blocks
    shape = jax.ShapeDtypeStruct
    smem = pl.BlockSpec(memory_space=pltpu.SMEM)
    vmem = pl.BlockSpec(memory_space=pltpu.VMEM)
    return pl.pallas_call(
        functools.partial(
            list_kernel, (part_blocks, half_blocks, total_blocks, slots, random)
        ),
        out_shape=[shape((slots, lanes), jnp.int32)] * 3
        + [shape((1, lanes), jnp.int32)]
        + [shape((half_blocks, lanes), jnp.int32)] * 2,
        in_specs=[smem, smem, vmem],
        out_specs=[vmem] * 6,
        name="key_lists",
    )(spot, doc_starts, picks)


def chunk_tile(rows, width):
    return lax.broadcasted_iota(jnp.int32, (rows, width), 1) // HEAD_DIM


def head_diag(tile, heads):
    owner = chunk_tile(BLOCK, heads * HEAD_DIM)
    return jnp.concatenate(
        [jnp.where(owner == head, tile, jnp.zeros_like(tile)) for head in range(heads)], axis=0
    )


def diag_rows(full, heads):
    owner = chunk_tile(BLOCK, heads * HEAD_DIM)
    picked = full[:BLOCK]
    for head in range(1, heads):
        picked = jnp.where(owner == head, full[head * BLOCK : (head + 1) * BLOCK], picked)
    return picked


def tile_bias(block, count, place_ref, base_ref, kind_ref, first_ref, end_ref):
    first = first_ref[pl.ds(block, 1), :]
    end = end_ref[pl.ds(block, 1), :]
    key = lax.broadcasted_iota(jnp.int32, (BLOCK, 2 * BLOCK), 0)
    starts = []
    biases = []
    for slot in range(count):
        starts.append(pl.multiple_of(place_ref[slot, block] * BLOCK, BLOCK))
        base = base_ref[slot, block]
        kind = kind_ref[slot, block]
        high = jnp.where(kind == 2, end, first + GLOBAL_BLOCKS * BLOCK)
        high = jnp.where(kind == 0, -1, high - base)
        allowed = (key >= first - base) & (key < high)
        biases.append(jnp.where(allowed, 0.0, masked_score))
    return starts, jnp.concatenate(biases, axis=0)


NT = (((1,), (1,)), ((), ()))
NN = (((1,), (0,)), ((), ()))
TN = (((0,), (0,)), ((), ()))


def gathered(pool_ref, starts, low, span):
    return jnp.concatenate(
        [pool_ref[pl.ds(start, BLOCK), low : low + span] for start in starts], axis=0
    )


def masked_scores(keys, query_diag, bias, heads):
    scores = lax.dot_general(keys, query_diag, NT, preferred_element_type=jnp.float32)
    return scores + jnp.concatenate([bias] * (heads // 2), axis=1)


def soft_columns(scores):
    top = jnp.max(scores, axis=0, keepdims=True)
    raised = jnp.exp(scores - top)
    total = jnp.sum(raised, axis=0, keepdims=True)
    return raised * (1.0 / total)


def load_pool(chunks, pool_ref, sems):
    rows = chunks[0].shape[0]
    copies = [
        pltpu.make_async_copy(chunk, pool_ref.at[pl.ds(n * rows, rows)], sems.at[n])
        for n, chunk in enumerate(chunks)
    ]
    for copy in copies:
        copy.start()
    return copies


def each_block(blocks, few, slots, count_ref, work):
    together = 2

    def step(n, carry):
        first = n * together
        short = count_ref[0, first] <= few
        for more in range(1, together):
            short = jnp.logical_and(short, count_ref[0, first + more] <= few)

        @pl.when(short)
        def _():
            work([first + more for more in range(together)], few)

        @pl.when(jnp.logical_not(short))
        def _():
            def single(more, carry):
                work([first + more], slots)
                return carry

            lax.fori_loop(0, together, single, 0)

        return carry

    lax.fori_loop(0, blocks // together, step, 0)


def split_store(source, kept, given, sems):
    rows = kept.shape[0]
    copies = [
        pltpu.make_async_copy(source.at[pl.ds(n * rows, rows)], target, sems.at[n])
        for n, target in enumerate((kept, given))
    ]
    for copy in copies:
        copy.start()
    for copy in copies:
        copy.wait()


def attend_kernel(sizes, *refs):
    blocks, slots, few, groups, width = sizes
    place_ref, base_ref, kind_ref, count_ref, first_ref, end_ref, query_ref = refs[:7]
    chunks = refs[7:-5]
    kept_ref, given_ref, out_ref, pool_ref, sems = refs[-5:]
    for copy in load_pool(chunks, pool_ref, sems):
        copy.wait()

    def work(chosen, count):
        tasks = []
        for block in chosen:
            starts, bias = tile_bias(
                block, count, place_ref, base_ref, kind_ref, first_ref, end_ref
            )
            here = pl.ds(pl.multiple_of(block * BLOCK, BLOCK), BLOCK)
            tasks += [(starts, bias, here, low, heads) for low, heads in groups]
        scores = []
        for starts, bias, here, low, heads in tasks:
            span = heads * HEAD_DIM
            query_diag = head_diag(query_ref[here, low : low + span], heads)
            keys = gathered(pool_ref, starts, low, span)
            scores.append(masked_scores(keys, query_diag, bias, heads))
        probs = [soft_columns(score).astype(jnp.bfloat16) for score in scores]
        for (starts, bias, here, low, heads), prob in zip(tasks, probs):
            span = heads * HEAD_DIM
            values = gathered(pool_ref, starts, width + low, span)
            mixed = lax.dot_general(prob, values, TN, preferred_element_type=jnp.float32)
            out_ref[here, low : low + span] = diag_rows(mixed, heads).astype(jnp.bfloat16)

    each_block(blocks, few, slots, count_ref, work)
    split_store(out_ref, kept_ref, given_ref, sems)


def attend_back_kernel(sizes, *refs):
    blocks, slots, few, groups, width, parts = sizes
    place_ref, base_ref, kind_ref, count_ref, first_ref, end_ref, query_ref = refs[:7]
    grad_parts = refs[7:9]
    chunks = refs[9 : 9 + parts]
    query_grads = refs[9 + parts : 11 + parts]
    outs = refs[11 + parts : 11 + 2 * parts]
    grad_ref, query_grad_ref, pool_ref, total_ref, sems = refs[11 + 2 * parts :]
    copies = load_pool(chunks, pool_ref, sems)
    rows = chunks[0].shape[0]
    for n, part in enumerate(grad_parts):
        copies.append(
            pltpu.make_async_copy(part, grad_ref.at[pl.ds(n * rows, rows)], sems.at[parts + n])
        )
        copies[-1].start()
    strip = 128

    def clear(n, carry):
        at = pl.ds(pl.multiple_of(n * strip, strip), strip)
        total_ref[at, :] = jnp.zeros((strip, 2 * width), jnp.float32)
        return carry

    lax.fori_loop(0, parts * rows // strip, clear, 0)
    for copy in copies:
        copy.wait()

    def work(chosen, count):
        tasks = []
        for block in chosen:
            starts, bias = tile_bias(
                block, count, place_ref, base_ref, kind_ref, first_ref, end_ref
            )
            here = pl.ds(pl.multiple_of(block * BLOCK, BLOCK), BLOCK)
            tasks += [(starts, bias, here, low, heads) for low, heads in groups]
        fronts = []
        for starts, bias, here, low, heads in tasks:
            span = heads * HEAD_DIM
            query_diag = head_diag(query_ref[here, low : low + span], heads)
            grad_diag = head_diag(grad_ref[here, low : low + span], heads)
            keys = gathered(pool_ref, starts, low, span)
            values = gathered(pool_ref, starts, width + low, span)
            scores = masked_scores(keys, query_diag, bias, heads)
            grad_probs = lax.dot_general(values, grad_diag, NT, preferred_element_type=jnp.float32)
            fronts.append((query_diag, grad_diag, keys, scores, grad_probs))
        for (starts, bias, here, low, heads), front in zip(tasks, fronts):
            query_diag, grad_diag, keys, scores, grad_probs = front
            span = heads * HEAD_DIM
            probs = soft_columns(scores)
            inner = jnp.sum(probs * grad_probs, axis=0, keepdims=True)
            grad_scores = (probs * (grad_probs - inner)).astype(jnp.bfloat16)
            grad_values = lax.dot_general(
                probs.astype(jnp.bfloat16), grad_diag, NN, preferred_element_type=jnp.float32
            )
            grad_keys = lax.dot_general(
                grad_scores, query_diag, NN, preferred_element_type=jnp.float32
            )
            grad_query = lax.dot_general(grad_scores, keys, TN, preferred_element_type=jnp.float32)
            query_grad_ref[here, low : low + span] = (
                diag_rows(grad_query, heads) * HEAD_DIM**-0.5
            ).astype(jnp.bfloat16)
            for slot, start in enumerate(starts):
                lines = slice(slot * BLOCK, (slot + 1) * BLOCK)
                total_ref[pl.ds(start, BLOCK), low : low + span] += grad_keys[lines]
                total_ref[pl.ds(start, BLOCK), width + low : width + low + span] += grad_values[
                    lines
                ]

    each_block(blocks, few, slots, count_ref, work)

    def lower(n, carry):
        at = pl.ds(pl.multiple_of(n * strip, strip), strip)
        pool_ref[at, :] = total_ref[at, :].astype(jnp.bfloat16)
        return carry

    split_store(query_grad_ref, *query_grads, sems)
    sends = []
    for n, out in enumerate(outs):
        lax.fori_loop(n * rows // strip, (n + 1) * rows // strip, lower, 0)
        send = pltpu.make_async_copy(pool_ref.at[pl.ds(n * rows, rows)], out, sems.at[n])
        send.start()
        sends.append(send)
    for send in sends:
        send.wait()


def attend(lists, query_rows, chunks, groups, slots, few):
    tokens, width = query_rows.shape
    rows = chunks[0].shape[0]
    parts = len(chunks)
    blocks = tokens // BLOCK
    smem = pl.BlockSpec(memory_space=pltpu.SMEM)
    vmem = pl.BlockSpec(memory_space=pltpu.VMEM)
    hbm = pl.BlockSpec(memory_space=pl.ANY)
    keys = few * BLOCK
    return pl.pallas_call(
        functools.partial(attend_kernel, (blocks, slots, few, groups, width)),
        out_shape=[jax.ShapeDtypeStruct((rows, width), jnp.bfloat16)] * 2,
        in_specs=[smem] * 4 + [vmem] * 3 + [hbm] * parts,
        out_specs=[hbm] * 2,
        scratch_shapes=[
            pltpu.VMEM((tokens, width), jnp.bfloat16),
            pltpu.VMEM((parts * rows, 2 * width), jnp.bfloat16),
            pltpu.SemaphoreType.DMA((parts,)),
        ],
        compiler_params=pltpu.CompilerParams(vmem_limit_bytes=VMEM_BYTES),
        cost_estimate=pl.CostEstimate(
            flops=16 * tokens * keys * width,
            bytes_accessed=4 * parts * rows * width,
            transcendentals=tokens * keys * width // HEAD_DIM,
        ),
        name="attend",
    )(*lists, query_rows, *chunks)


def attend_back(lists, query_rows, grad_parts, chunks, groups, slots, few):
    tokens, width = query_rows.shape
    rows = chunks[0].shape[0]
    parts = len(chunks)
    blocks = tokens // BLOCK
    smem = pl.BlockSpec(memory_space=pltpu.SMEM)
    vmem = pl.BlockSpec(memory_space=pltpu.VMEM)
    hbm = pl.BlockSpec(memory_space=pl.ANY)
    keys = few * BLOCK
    return pl.pallas_call(
        functools.partial(attend_back_kernel, (blocks, slots, few, groups, width, parts)),
        out_shape=[jax.ShapeDtypeStruct((rows, width), jnp.bfloat16)] * 2
        + [jax.ShapeDtypeStruct((rows, 2 * width), jnp.bfloat16)] * parts,
        in_specs=[smem] * 4 + [vmem] * 3 + [hbm] * (2 + parts),
        out_specs=[hbm] * (2 + parts),
        scratch_shapes=[
            pltpu.VMEM((tokens, width), jnp.bfloat16),
            pltpu.VMEM((tokens, width), jnp.bfloat16),
            pltpu.VMEM((parts * rows, 2 * width), jnp.bfloat16),
            pltpu.VMEM((parts * rows, 2 * width), jnp.float32),
            pltpu.SemaphoreType.DMA((parts + 2,)),
        ],
        compiler_params=pltpu.CompilerParams(vmem_limit_bytes=VMEM_BYTES),
        cost_estimate=pl.CostEstimate(
            flops=40 * tokens * keys * width,
            bytes_accessed=8 * parts * rows * width,
            transcendentals=tokens * keys * width // HEAD_DIM,
        ),
        name="attend_back",
    )(*lists, query_rows, *grad_parts, *chunks)


def row_norm(wide):
    mean = jnp.mean(wide, axis=-1, keepdims=True)
    centred = wide - mean
    inverse = lax.rsqrt(jnp.mean(centred * centred, axis=-1, keepdims=True) + layer_eps)
    return centred * inverse, inverse


def row_norm_back(grad, normal, inverse):
    mean = jnp.mean(grad, axis=-1, keepdims=True)
    along = jnp.mean(grad * normal, axis=-1, keepdims=True)
    return inverse * (grad - mean - normal * along)


def normal_parts(wide):
    size = jnp.abs(wide)
    bell = jnp.exp(-0.5 * wide * wide)
    step = 1.0 / (1.0 + (0.3275911 * math.sqrt(0.5)) * size)
    poly = 0.5 * 1.061405429
    for factor in (-1.453152027, 1.421413741, -0.284496736, 0.254829592):
        poly = poly * step + 0.5 * factor
    tail = poly * step * bell
    return jnp.where(wide < 0, tail, 1.0 - tail), bell * (1.0 / math.sqrt(2 * math.pi))


def column_sum(wide):
    return jnp.sum(wide, axis=0, keepdims=True)


def dense_kernel(sizes, *refs):
    tile, piece = sizes
    spot_ref, kept_ref, given_ref, input_ref, top_ref, vector_ref, offset_ref = refs[:7]
    weights = refs[7]
    out_ref, first_ref, grad_kept_ref, grad_given_ref, line_ref, hidden_line_ref = refs[8:14]
    grads = refs[14]
    expand_ref, mixer_ref, shrink_ref = refs[15:18]
    active_ref, pre_grad_ref, slope_ref = refs[18:21]
    middle_ref, ffn_ref, branch_ref, sems = refs[21:]
    bf16 = jnp.bfloat16
    f32 = jnp.float32
    tokens, width = input_ref.shape
    half = width // 2
    hidden = expand_ref.shape[1]
    core = spot_ref[1]
    fold = hidden // width

    def dot(left, right, kind):
        return lax.dot_general(left, right, kind, preferred_element_type=f32)

    places = [(mixer_ref, hidden, width), (expand_ref, 0, hidden)]
    for block in range(fold):
        part = shrink_ref.at[pl.ds(block * width, width)]
        places.append((part, hidden + (1 + block) * width, width))
    loads = [
        pltpu.make_async_copy(weights.at[:, pl.ds(low, span)], part, sems.at[n])
        for n, (part, low, span) in enumerate(places)
    ]
    for load in loads:
        load.start()
    for load in loads:
        load.wait()

    line_ref[...] = jnp.zeros_like(line_ref)
    hidden_line_ref[...] = jnp.zeros_like(hidden_line_ref)
    vector = [vector_ref[pl.ds(n, 1), :] for n in range(8)]
    _, _, mixer_bias, first_gain, first_shift, shrink_bias, second_gain, second_shift = vector
    kept_rows = pl.ds(pl.multiple_of(core * half, half), half)
    given_rows = pl.ds(pl.multiple_of((1 - core) * half, half), half)

    def step(n, carry):
        at = pl.ds(pl.multiple_of(n * tile, tile), tile)
        first_sum = input_ref[at, :].astype(f32) + (
            dot(kept_ref[at, :], mixer_ref[kept_rows, :], NN)
            + dot(given_ref[at, :], mixer_ref[given_rows, :], NN)
            + mixer_bias
        )
        first_normal, first_inverse = row_norm(first_sum)
        middle = first_normal * first_gain + first_shift
        middle_low = middle.astype(bf16)
        middle_ref[at, :] = middle_low
        second_sum = middle + shrink_bias
        for low in range(0, hidden, piece):
            span = slice(low, low + piece)
            pre = dot(middle_low, expand_ref[:, span], NN) + offset_ref[:, span]
            share, density = normal_parts(pre)
            active = (pre * share).astype(bf16)
            active_ref[at, span] = active
            slope_ref[:, span] = share + pre * density
            second_sum = second_sum + dot(active, shrink_ref[span, :], NN)
        second_normal, second_inverse = row_norm(second_sum)
        out_ref[at, :] = (second_normal * second_gain + second_shift).astype(bf16)
        top = top_ref[at, :].astype(f32)
        second = row_norm_back(top * second_gain, second_normal, second_inverse)
        ffn = second.astype(bf16)
        ffn_ref[at, :] = ffn
        middle_grad = second
        for low in range(0, hidden, piece):
            span = slice(low, low + piece)
            pre_grad = dot(ffn, shrink_ref[span, :], NT) * slope_ref[:, span]
            pre_low = pre_grad.astype(bf16)
            pre_grad_ref[at, span] = pre_low
            hidden_line_ref[:, span] += column_sum(pre_low.astype(f32))
            middle_grad = middle_grad + dot(pre_low, expand_ref[:, span], NT)
        first = row_norm_back(middle_grad * first_gain, first_normal, first_inverse)
        first_ref[at, :] = first
        branch = first.astype(bf16)
        branch_ref[at, :] = branch
        grad_kept_ref[at, :] = dot(branch, mixer_ref[kept_rows, :], NT).astype(bf16)
        grad_given_ref[at, :] = dot(branch, mixer_ref[given_rows, :], NT).astype(bf16)
        sums = [
            column_sum(branch.astype(f32)),
            column_sum(middle_grad * first_normal),
            column_sum(middle_grad),
            column_sum(ffn.astype(f32)),
            column_sum(top * second_normal),
            column_sum(top),
        ]
        for line, row in enumerate(sums):
            line_ref[pl.ds(2 + line, 1), :] += row
        return carry

    lax.fori_loop(0, tokens // tile, step, 0)

    stores = []

    def leave(slot):
        part, low, span = places[slot]
        stores.append(pltpu.make_async_copy(part, grads.at[:, pl.ds(low, span)], sems.at[slot]))
        stores[-1].start()

    strip = 384

    def shrink_step(n, carry):
        span = pl.ds(pl.multiple_of(n * strip, strip), strip)
        shrink_ref[span, :] = dot(active_ref[:, span], ffn_ref[...], TN).astype(bf16)
        return carry

    lax.fori_loop(0, hidden // strip, shrink_step, 0)
    for block in range(fold):
        leave(2 + block)
    for row in range(0, width, strip):
        rows = slice(row, row + strip)

        def expand_step(n, carry):
            span = pl.ds(pl.multiple_of(n * 2 * strip, 2 * strip), 2 * strip)
            expand_ref[rows, span] = dot(middle_ref[:, rows], pre_grad_ref[:, span], TN).astype(bf16)
            return carry

        lax.fori_loop(0, hidden // (2 * strip), expand_step, 0)
    leave(1)
    mixer_ref[kept_rows, :] = dot(kept_ref[...], branch_ref[...], TN).astype(bf16)
    mixer_ref[given_rows, :] = dot(given_ref[...], branch_ref[...], TN).astype(bf16)
    leave(0)
    for store in stores:
        store.wait()


def dense(spot, kept, given, inputs, top, vector_rows, hidden_offset, weights):
    tokens, width = inputs.shape
    hidden = hidden_offset.shape[1]
    fold = hidden // width
    tile = 256
    piece = 768
    bf16 = jnp.bfloat16
    f32 = jnp.float32
    smem = pl.BlockSpec(memory_space=pltpu.SMEM)
    vmem = pl.BlockSpec(memory_space=pltpu.VMEM)
    hbm = pl.BlockSpec(memory_space=pl.ANY)
    shape = jax.ShapeDtypeStruct
    return pl.pallas_call(
        functools.partial(dense_kernel, (tile, piece)),
        out_shape=[
            shape((tokens, width), bf16),
            shape((tokens, width), f32),
            shape((tokens, width // 2), bf16),
            shape((tokens, width // 2), bf16),
            shape((8, width), f32),
            shape((1, hidden), f32),
            shape(weights.shape, bf16),
        ],
        in_specs=[smem] + [vmem] * 6 + [hbm],
        out_specs=[vmem] * 6 + [hbm],
        scratch_shapes=[
            pltpu.VMEM((width, hidden), bf16),
            pltpu.VMEM((width, width), bf16),
            pltpu.VMEM((hidden, width), bf16),
            pltpu.VMEM((tokens, hidden), bf16),
            pltpu.VMEM((tokens, hidden), bf16),
            pltpu.VMEM((tile, hidden), f32),
            pltpu.VMEM((tokens, width), bf16),
            pltpu.VMEM((tokens, width), bf16),
            pltpu.VMEM((tokens, width), bf16),
            pltpu.SemaphoreType.DMA((2 + fold,)),
        ],
        compiler_params=pltpu.CompilerParams(vmem_limit_bytes=VMEM_BYTES),
        cost_estimate=pl.CostEstimate(
            flops=6 * tokens * width * (2 * hidden + width),
            bytes_accessed=8 * width * (2 * hidden + width),
            transcendentals=2 * tokens * hidden,
        ),
        name="dense",
    )(spot, kept, given, inputs, top, vector_rows, hidden_offset, weights)


def table_kernel(sizes, *refs):
    counts, half = sizes
    chunks = len(counts)
    spot_ref = refs[0]
    pieces = refs[1 : 1 + sum(counts)]
    refs = refs[1 + sum(counts) :]
    pair_grads = refs[:chunks]
    query_grads = refs[chunks : chunks + 2]
    stay_ref, leave_ref, line_ref = refs[chunks + 2 : chunks + 5]
    total_ref, rows_ref, grads_ref, query_ref, sems = refs[chunks + 5 :]
    core = spot_ref[1]
    width = rows_ref.shape[2]
    f32 = jnp.float32

    def fetch(n):
        slot = n % 2
        copies = []
        low = 0
        for piece in pieces[sum(counts[:n]) : sum(counts[: n + 1])]:
            target = rows_ref.at[slot, pl.ds(low, piece.shape[0])]
            copies.append(pltpu.make_async_copy(piece, target, sems.at[slot, len(copies)]))
            low += piece.shape[0]
        copies.append(pltpu.make_async_copy(pair_grads[n], grads_ref.at[slot], sems.at[slot, 2]))
        if n < 2:
            copies.append(
                pltpu.make_async_copy(query_grads[n], query_ref.at[slot], sems.at[slot, 3])
            )
        for copy in copies:
            copy.start()
        return copies

    line_ref[...] = jnp.zeros_like(line_ref)
    waiting = fetch(0)
    step = 384
    for n in range(chunks):
        following = fetch(n + 1) if n + 1 < chunks else []
        for copy in waiting:
            copy.wait()
        slot = n % 2
        for row in range(0, width, step):
            rows = rows_ref[slot, :, row : row + step]
            here = slice(row, row + step)
            for column in range(0, 2 * half, step):
                there = slice(column, column + step)
                part = lax.dot_general(
                    rows, grads_ref[slot, :, there], TN, preferred_element_type=f32
                )
                total_ref[here, there] = part if n == 0 else total_ref[here, there] + part
            if n < 2:
                there = slice(2 * half, 3 * half)
                part = lax.dot_general(rows, query_ref[slot], TN, preferred_element_type=f32)
                total_ref[here, there] = part if n == 0 else total_ref[here, there] + part
        line_ref[pl.ds(0, 1), :] += jnp.sum(
            grads_ref[slot, :, half:].astype(f32), axis=0, keepdims=True
        )
        if n < 2:
            line_ref[pl.ds(1, 1), :] += jnp.sum(
                query_ref[slot].astype(f32), axis=0, keepdims=True
            )
        waiting = following
    lines = width // 4
    for side in range(2):
        for away, out in enumerate((stay_ref, leave_ref)):
            at = pl.ds(pl.multiple_of((2 * side + (core ^ away)) * lines, 64), lines)
            out[side] = total_ref[at, :].astype(out.dtype)


def table_grads(spot, rows_in, pair_grads, query_grads):
    smem = pl.BlockSpec(memory_space=pltpu.SMEM)
    vmem = pl.BlockSpec(memory_space=pltpu.VMEM)
    hbm = pl.BlockSpec(memory_space=pl.ANY)
    counts = tuple(len(pieces) for pieces in rows_in)
    flat = [piece for pieces in rows_in for piece in pieces]
    rows, total = pair_grads[0].shape
    half = total // 2
    width = flat[0].shape[1]
    bf16 = jnp.bfloat16
    shape = jax.ShapeDtypeStruct
    return pl.pallas_call(
        functools.partial(table_kernel, (counts, half)),
        out_shape=[
            shape((2, width // 4, 3 * half), jnp.float32),
            shape((2, width // 4, 3 * half), bf16),
            shape((8, half), jnp.float32),
        ],
        in_specs=[smem] + [hbm] * (len(flat) + len(pair_grads) + 2),
        out_specs=[vmem] * 3,
        scratch_shapes=[
            pltpu.VMEM((width, 3 * half), jnp.float32),
            pltpu.VMEM((2, rows, width), bf16),
            pltpu.VMEM((2, rows, total), bf16),
            pltpu.VMEM((2, rows, half), bf16),
            pltpu.SemaphoreType.DMA((2, 4)),
        ],
        compiler_params=pltpu.CompilerParams(vmem_limit_bytes=VMEM_BYTES),
        cost_estimate=pl.CostEstimate(flops=10**10, bytes_accessed=4 * 10**7, transcendentals=0),
        name="table_grads",
    )(spot, *flat, *pair_grads, *query_grads)


def pick(flag, first, second):
    return jnp.where(flag == 0, first, second)


def split_low(wide, width):
    high = lax.reduce_precision(wide, 8, 7)
    parts = [high.astype(jnp.bfloat16), (wide - high).astype(jnp.bfloat16)]
    pad = width - 2 * wide.shape[-1]
    parts.append(jnp.zeros(wide.shape[:-1] + (pad,), jnp.bfloat16))
    return jnp.concatenate(parts, axis=-1)


def join_low(packed, count):
    wide = packed.astype(jnp.float32)
    return wide[..., :count] + wide[..., count : 2 * count]


def body(
    tokens_in,
    query_weight,
    query_bias,
    key_weight,
    value_weight,
    value_bias,
    mixer_weight,
    mixer_bias,
    first_gain,
    first_shift,
    expand_weight,
    expand_bias,
    shrink_weight,
    shrink_bias,
    second_gain,
    second_shift,
    doc_starts,
    random_blocks,
    cotangent,
):
    f32 = jnp.float32
    bf16 = jnp.bfloat16
    axes = ("head", "blk")
    head_count = lax.axis_size("head")
    cycle_size = lax.axis_size("blk")
    devices = head_count * cycle_size
    head_index = lax.axis_index("head")
    cycle_index = lax.axis_index("blk")
    side = head_index // 2
    core = head_index % 2
    level = cycle_index // 2
    turn = cycle_index % 2
    levels = cycle_size // 2
    local_rows = tokens_in.shape[1]
    model_width = tokens_in.shape[2]
    half_width = model_width // 2
    hidden = expand_weight.shape[1]
    fold = hidden // model_width
    own_rows = query_weight.shape[0]
    part_blocks = local_rows // BLOCK
    half_blocks = 2 * part_blocks
    total_blocks = part_blocks * devices
    slots = 3 + random_blocks.shape[1] + 2 * (GLOBAL_BLOCKS + 1)
    few = slots - GLOBAL_BLOCKS - 1
    groups = ((0, 4), (4 * HEAD_DIM, 2))

    def flat(head, cycle):
        return head * cycle_size + cycle

    everywhere = [(h, b) for h in range(head_count) for b in range(cycle_size)]
    over_side = [(flat(h, b), flat(h ^ 2, b)) for h, b in everywhere]
    over_core = [(flat(h, b), flat(h ^ 1, b)) for h, b in everywhere]
    over_turn = [(flat(h, b), flat(h, b ^ 1)) for h, b in everywhere]
    inward = [
        (flat(h, b), flat(h, b + (1 if h >= 2 else -1)))
        for h, b in everywhere
        if 0 <= b + (1 if h >= 2 else -1) < cycle_size
    ]
    outward = [
        (flat(h, b), flat(h, b + (-1 if h >= 2 else 1)))
        for h, b in everywhere
        if 0 <= b + (-1 if h >= 2 else 1) < cycle_size
    ]

    def send(array, pairs):
        return lax.ppermute(array, axes, pairs)

    def send_back(array, pairs):
        return lax.ppermute(array, axes, [(b, a) for a, b in pairs])

    spans = [1 << n for n in range(levels.bit_length() - 1)]
    together = lax.optimization_barrier

    def over_level(span):
        return [(flat(h, b), flat(h, b ^ (2 * span))) for h, b in everywhere]

    def joined(flag, own, other, axis):
        return pick(flag, jnp.stack([own, other], axis), jnp.stack([other, own], axis))

    half_index = 2 * cycle_index + side
    spot = jnp.stack([side, core, half_index]).astype(jnp.int32)

    vectors = [
        query_bias,
        value_bias,
        mixer_bias,
        first_gain,
        first_shift,
        shrink_bias,
        second_gain,
        second_shift,
    ]
    line_count = len(vectors) + fold
    line_width = 128
    per_row = -(-(len(vectors) + 1) // own_rows)
    gap = line_width // per_row
    shard = pack(
        key_weight, value_weight, query_weight, vectors + [expand_bias], per_row, gap
    )
    trio = 3 * half_width
    wide_columns = hidden + model_width
    rest_shard = jnp.concatenate(
        [
            expand_weight.reshape(own_rows, model_width, fold)
            .transpose(0, 2, 1)
            .reshape(own_rows, hidden),
            mixer_weight,
            shrink_weight.reshape(own_rows, hidden),
        ],
        axis=1,
    ).astype(bf16)

    latest = []

    def turn_for(array):
        return together((array, latest[-1]))[0] if latest else array

    def mark(array):
        latest.append(array)
        return array

    def done(array):
        return mark(turn_for(array))

    inputs = tokens_in[0]
    beside = send(inputs, over_side)
    near = send(inputs, inward)
    tables = lax.all_gather(shard, axes, axis=0, tiled=True)
    rest = lax.all_gather(together((rest_shard, shard))[0], axes, axis=0, tiled=True)
    inputs_other = send(inputs, over_core)
    inputs_other = done(inputs_other)
    near = done(near)
    passed = send(near, over_side)
    far = send(together((inputs, near))[0], outward)
    beside = done(beside)
    near_other = send(near, over_core)
    near_other = done(near_other)
    beside_other = send(together((beside, near_other))[0], over_core)
    beside_other = done(beside_other)
    tables = done(tables)
    table = jnp.concatenate(
        [pick(core, tables[:, :trio], tables[:, trio : 2 * trio]), tables[:, 2 * trio :]], axis=1
    )

    pair_matrix = table[:, :model_width]
    query_matrix = table[:, model_width:trio]
    every_line = table[:, trio:].astype(f32).reshape(devices, own_rows, line_width)

    def line_of(n, size):
        low = n % per_row * gap
        return every_line[:, n // per_row, low : low + size].reshape(devices * size)

    vector_rows = jnp.stack([line_of(n, own_rows) for n in range(len(vectors))])
    expand_offset = line_of(len(vectors), own_rows * fold)
    expand_offset = expand_offset.reshape(model_width, fold).T.reshape(1, hidden)
    query_offset = pick(core, vector_rows[0, :half_width], vector_rows[0, half_width:])
    value_offset = pick(core, vector_rows[1, :half_width], vector_rows[1, half_width:])
    pair_offset = jnp.concatenate([jnp.zeros((half_width,), f32), value_offset])
    picks = jnp.concatenate(
        [
            lax.dynamic_slice_in_dim(random_blocks, head_index * part_blocks, part_blocks),
            lax.dynamic_slice_in_dim(random_blocks, (head_index ^ 1) * part_blocks, part_blocks),
        ],
        axis=0,
    ).T
    picks = jnp.pad(picks, ((0, 0), (0, 2 * BLOCK - half_blocks)))
    lists = key_lists(
        spot, doc_starts, picks, part_blocks, total_blocks, slots, random_blocks.shape[1]
    )

    def project(rows, matrix, offset):
        return (jnp.dot(rows, matrix, preferred_element_type=f32) + offset).astype(bf16)

    def project_pair(rows):
        return project(rows, pair_matrix, pair_offset)

    query_rows = jnp.concatenate(
        [project(turn_for(rows), query_matrix, query_offset) for rows in (inputs, inputs_other)],
        axis=0,
    ) * jnp.asarray(HEAD_DIM**-0.5, bf16)
    mark(query_rows)
    rows_in = [[inputs], [inputs_other], [beside], [beside_other], [near], [near_other]]
    chunks = [mark(project_pair(turn_for(rows))) for (rows,) in rows_in]
    passed = done(passed)
    passed_other = send(passed, over_core)
    far = done(far)
    far_other = send(far, over_core)
    chunks.append(mark(project_pair(turn_for(passed))))
    passed_other = done(passed_other)
    chunks.append(mark(project_pair(passed_other)))
    chunks.append(mark(project_pair(turn_for(far))))
    far_other = done(far_other)
    chunks.append(mark(project_pair(far_other)))
    rows_in += [[passed], [passed_other], [far], [far_other]]
    mixed_kept, mixed_leaving = attend(lists, query_rows, chunks, groups, slots, few)
    mark(mixed_leaving)
    mixed_given = send(mixed_leaving, over_core)
    (
        layer_out,
        grad_first,
        grad_kept,
        grad_leaving,
        dense_lines,
        hidden_line,
        rest_grad,
    ) = dense(
        spot,
        mixed_kept,
        mixed_given,
        inputs,
        cotangent[0],
        vector_rows,
        expand_offset,
        rest,
    )
    mark(grad_leaving)
    grad_given = send(grad_leaving, over_core)
    rest_total = lax.psum_scatter(rest_grad, axes, scatter_dimension=0, tiled=True)
    pair_grads = attend_back(
        lists, query_rows, (grad_kept, grad_given), chunks, groups, slots, few
    )
    query_grads = pair_grads[:2]
    pair_grads = pair_grads[2:]

    def halves(array, flag, axis):
        return [
            lax.dynamic_index_in_dim(array, index, axis, keepdims=False)
            for index in (flag, 1 - flag)
        ]

    mark(query_grads[0])

    def back(grad, matrix):
        return jnp.einsum("te,de->td", turn_for(grad), matrix, preferred_element_type=f32)

    def leave(n):
        total = back(pair_grads[2 * n + 1], pair_matrix)
        if n == 0:
            total = total + back(query_grads[1], query_matrix)
        return send(mark(total.astype(bf16)), over_core)

    def stay(n, *extras):
        total = back(pair_grads[2 * n], pair_matrix)
        for extra in extras:
            total = total + extra.astype(f32)
        return mark(total.astype(bf16))

    passed_given = leave(3)
    far_given = leave(4)
    passed_given = done(passed_given)
    passed_back = send(stay(3, passed_given), over_side)
    far_given = done(far_given)
    far_back = send_back(stay(4, far_given), outward)
    near_given = leave(2)
    beside_given = leave(1)
    near_given = done(near_given)
    beside_given = done(beside_given)
    beside_back = send(stay(1, beside_given), over_side)
    own_given = leave(0)
    table_stay, table_leave, half_lines = table_grads(
        spot, rows_in, pair_grads, [turn_for(grad) for grad in query_grads]
    )
    mark(half_lines)
    own_given = done(own_given)
    table_given = send(table_leave, over_core)
    passed_back = done(passed_back)
    near_back = send_back(stay(2, near_given, passed_back), inward)
    table_given = done(table_given)

    def placed(half_row):
        nothing = jnp.zeros_like(half_row)
        return pick(
            core,
            jnp.concatenate([half_row, nothing], axis=1),
            jnp.concatenate([nothing, half_row], axis=1),
        )

    line_rows = jnp.concatenate(
        [
            placed(half_lines[1:2]),
            placed(half_lines[0:1]),
            dense_lines[2:],
            hidden_line.reshape(fold, model_width),
        ],
        axis=0,
    )
    line_sum = line_rows.T.reshape(2, 2, cycle_size * own_rows, line_count)

    def pack_lines(lines):
        return split_low(lines, line_width)

    def joined_columns(own, other):
        return pick(
            core,
            jnp.concatenate([own, other], axis=2),
            jnp.concatenate([other, own], axis=2),
        )

    line_halves = halves(line_sum, core, 1)
    line_given = send(pack_lines(line_halves[1]), over_core)
    columns = 2 * trio
    table_given = table_given.astype(f32)
    table_sum = joined_columns(table_stay, table_given)
    line_sum = line_halves[0] + join_low(line_given, line_count)

    def table_step(tables, lines, pairs):
        leaving = jnp.concatenate([tables[1].astype(bf16), pack_lines(lines[1])], axis=-1)
        return send(mark(leaving), pairs)

    def table_add(tables, lines, arrived):
        arrived = turn_for(arrived)
        return (
            tables[0] + arrived[..., :columns].astype(f32),
            lines[0] + join_low(arrived[..., columns:], line_count),
        )

    tables, lines = halves(table_sum, side, 0), halves(line_sum, side, 0)
    table_arrived = table_step(tables, lines, over_side)
    far_back = done(far_back)
    own_total = mark(
        grad_first
        + back(pair_grads[0], pair_matrix)
        + back(query_grads[0], query_matrix)
        + own_given.astype(f32)
        + far_back.astype(f32)
    )
    table_sum, line_sum = table_add(tables, lines, table_arrived)
    table_sum = table_sum.reshape(levels, 2, own_rows, columns)
    line_sum = line_sum.reshape(levels, 2, own_rows, line_count)
    tables, lines = halves(table_sum, turn, 1), halves(line_sum, turn, 1)
    table_arrived = table_step(tables, lines, over_turn)
    rest_total = done(rest_total).astype(f32)
    for span in spans:
        table_sum, line_sum = table_add(tables, lines, table_arrived)
        flag = (level // span) % 2
        tables = halves(table_sum.reshape((-1, 2) + table_sum.shape[1:]), flag, 1)
        lines = halves(line_sum.reshape((-1, 2) + line_sum.shape[1:]), flag, 1)
        table_arrived = table_step(tables, lines, over_level(span))
    table_sum, line_sum = table_add(tables, lines, table_arrived)
    table_own = table_sum[0]
    line_own = line_sum[0]
    input_grad = own_total + beside_back.astype(f32) + near_back.astype(f32)

    def columns_of(which):
        low = which * half_width
        return jnp.concatenate(
            [table_own[:, low : low + half_width], table_own[:, trio + low : trio + low + half_width]],
            axis=1,
        )

    return (
        layer_out[None],
        input_grad[None],
        columns_of(2),
        line_own[:, 0],
        columns_of(0),
        columns_of(1),
        line_own[:, 1],
        rest_total[:, hidden:wide_columns],
        line_own[:, 2],
        line_own[:, 3],
        line_own[:, 4],
        rest_total[:, :hidden]
        .reshape(own_rows, fold, model_width)
        .transpose(0, 2, 1)
        .reshape(own_rows, hidden),
        line_own[:, len(vectors) :].reshape(-1),
        rest_total[:, wide_columns:].reshape(own_rows * fold, model_width),
        line_own[:, 5],
        line_own[:, 6],
        line_own[:, 7],
    )


def solution(mesh):
    in_specs = (
        P("blk", "head", None),
        P(("head", "blk"), None),
        P(("head", "blk")),
        P(("head", "blk"), None),
        P(("head", "blk"), None),
        P(("head", "blk")),
        P(("head", "blk"), None),
        P(("head", "blk")),
        P(("head", "blk")),
        P(("head", "blk")),
        P(("head", "blk"), None),
        P(("head", "blk")),
        P(("head", "blk"), None),
        P(("head", "blk")),
        P(("head", "blk")),
        P(("head", "blk")),
        P(),
        P("blk", None),
        P("blk", "head", None),
    )
    out_specs = (
        P("blk", "head", None),
        P("blk", "head", None),
        P(("head", "blk"), None),
        P(("head", "blk")),
        P(("head", "blk"), None),
        P(("head", "blk"), None),
        P(("head", "blk")),
        P(("head", "blk"), None),
        P(("head", "blk")),
        P(("head", "blk")),
        P(("head", "blk")),
        P(("head", "blk"), None),
        P(("head", "blk")),
        P(("head", "blk"), None),
        P(("head", "blk")),
        P(("head", "blk")),
        P(("head", "blk")),
    )
    return jax.shard_map(body, mesh=mesh, in_specs=in_specs, out_specs=out_specs, check_vma=False)
```

```python
import functools
import math

import jax
import jax.numpy as jnp
from jax import lax
from jax.experimental import pallas as pl
from jax.experimental.pallas import tpu as pltpu
from jax.sharding import PartitionSpec as P

HEADS = 12
HEAD_DIM = 64
BLOCK = 64
GLOBAL_BLOCKS = 2
MAXDOC = 4096
VMEM_BYTES = 60 * 2**20

layer_eps = 1e-12
masked_score = -1e30

def pack_kernel(sizes, *refs):
    half, per_row, gap = sizes
    key_ref, value_ref, query_ref = refs[:3]
    vectors = refs[3:-1]
    out_ref = refs[-1]
    rows, total = out_ref.shape
    bf16 = jnp.bfloat16
    for n, source in enumerate((key_ref, value_ref, query_ref)):
        for core in range(2):
            at = (3 * core + n) * half
            out_ref[:, at : at + half] = source[:, core * half : (core + 1) * half].astype(bf16)
    line = lax.broadcasted_iota(jnp.int32, (rows, 128), 0)
    block = jnp.zeros((rows, 128), jnp.float32)
    for n, vector in enumerate(vectors):
        row = vector[...]
        low = n % per_row * gap
        pieces = [row, jnp.zeros((1, 128 - low - row.shape[1]), jnp.float32)]
        if low:
            pieces = [jnp.zeros((1, low), jnp.float32)] + pieces
        block = jnp.where(line == n // per_row, block + jnp.concatenate(pieces, axis=1), block)
    out_ref[:, 6 * half :] = block.astype(bf16)


def pack(key_weight, value_weight, query_weight, vectors, per_row, gap):
    rows, width = key_weight.shape
    vmem = pl.BlockSpec(memory_space=pltpu.VMEM)
    return pl.pallas_call(
        functools.partial(pack_kernel, (width // 2, per_row, gap)),
        out_shape=jax.ShapeDtypeStruct((rows, 3 * width + 128), jnp.bfloat16),
        in_specs=[vmem] * (3 + len(vectors)),
        out_specs=vmem,
        name="pack",
    )(key_weight, value_weight, query_weight, *[vector[None] for vector in vectors])


def list_kernel(sizes, spot_ref, starts_ref, picks_ref, *outs):
    place_ref, base_ref, kind_ref, count_ref, first_ref, end_ref = outs
    part_blocks, half_blocks, total_blocks, slots, random = sizes
    bits = BLOCK.bit_length() - 1
    part_bits = part_blocks.bit_length() - 1
    half_bits = half_blocks.bit_length() - 1
    lanes = 2 * BLOCK
    side, core, half_index = [spot_ref[n] for n in range(3)]
    docs = [starts_ref[n] for n in range(starts_ref.shape[0])]
    int32 = jnp.int32

    def block_of(n):
        part = jnp.where(n < part_blocks, core, 1 - core)
        return half_index * half_blocks + part * part_blocks + (n & (part_blocks - 1))

    def first_of(position):
        first = jnp.zeros(position.shape, int32)
        for start in docs:
            first = jnp.where(position >= start, start, first)
        return first

    def end_of(position):
        end = jnp.full(position.shape, total_blocks * BLOCK, int32)
        for start in docs[::-1]:
            end = jnp.where(position < start, start, end)
        return end

    rows = lax.broadcasted_iota(int32, (half_blocks, lanes), 0)
    columns = lax.broadcasted_iota(int32, (half_blocks, lanes), 1)
    positions = block_of(rows) * BLOCK + (columns & (BLOCK - 1))
    first_ref[...] = first_of(positions)
    end_ref[...] = end_of(positions)

    block = block_of(lax.broadcasted_iota(int32, (1, lanes), 1))
    lead = block * BLOCK
    first_lead = first_of(lead)
    first_tail = first_of(lead + BLOCK - 1)
    end_tail = end_of(lead + BLOCK - 1)
    picks = [picks_ref[pl.ds(n, 1), :] for n in range(random)]
    candidates = [block - 1, block, block + 1] + picks
    for anchor in (first_lead, first_tail):
        candidates += [(anchor >> bits) + offset for offset in range(GLOBAL_BLOCKS + 1)]
    candidates = [jnp.clip(candidate, 0, total_blocks - 1) for candidate in candidates]
    seated = [[jnp.zeros((1, lanes), int32)] * 3 for _ in range(slots)]
    rank = jnp.zeros((1, lanes), int32)
    for n, candidate in enumerate(candidates):
        useful = candidate >= 0
        for earlier in candidates[:n]:
            useful = useful & (candidate != earlier)
        nearby = jnp.abs(candidate - block) <= 1
        for chosen in picks:
            nearby = nearby | (candidate == chosen)
        base = candidate * BLOCK
        useful = useful & (base + BLOCK > first_lead) & (base < end_tail)
        useful = useful & (nearby | (base < first_tail + GLOBAL_BLOCKS * BLOCK))
        apart = (candidate >> half_bits) - half_index
        reach = jnp.abs(apart)
        useful = useful & (reach <= 2)
        later = (apart > 0).astype(int32)
        slot = jnp.where(later == 1 - side, reach, reach + 2)
        slot = jnp.where(reach == 0, 0, slot)
        part = ((candidate >> part_bits) & 1) ^ core
        place = (2 * slot + part) * part_blocks + (candidate & (part_blocks - 1))
        values = (place, base, 1 + nearby.astype(int32))
        for seat in range(n + 1):
            here = useful & (rank == seat)
            seated[seat] = [jnp.where(here, new, old) for new, old in zip(values, seated[seat])]
        rank = rank + useful.astype(int32)
    for seat in range(slots):
        for out, value in zip((place_ref, base_ref, kind_ref), seated[seat]):
            out[pl.ds(seat, 1), :] = value
    count_ref[...] = rank


def key_lists(spot, doc_starts, picks, part_blocks, total_blocks, slots, random):
    lanes = 2 * BLOCK
    half_blocks = 2 * part_blocks
    shape = jax.ShapeDtypeStruct
    smem = pl.BlockSpec(memory_space=pltpu.SMEM)
    vmem = pl.BlockSpec(memory_space=pltpu.VMEM)
    return pl.pallas_call(
        functools.partial(
            list_kernel, (part_blocks, half_blocks, total_blocks, slots, random)
        ),
        out_shape=[shape((slots, lanes), jnp.int32)] * 3
        + [shape((1, lanes), jnp.int32)]
        + [shape((half_blocks, lanes), jnp.int32)] * 2,
        in_specs=[smem, smem, vmem],
        out_specs=[vmem] * 6,
        name="key_lists",
    )(spot, doc_starts, picks)


def chunk_tile(rows, width):
    return lax.broadcasted_iota(jnp.int32, (rows, width), 1) // HEAD_DIM


def head_diag(tile, heads):
    owner = chunk_tile(BLOCK, heads * HEAD_DIM)
    return jnp.concatenate(
        [jnp.where(owner == head, tile, jnp.zeros_like(tile)) for head in range(heads)], axis=0
    )


def diag_rows(full, heads):
    owner = chunk_tile(BLOCK, heads * HEAD_DIM)
    picked = full[:BLOCK]
    for head in range(1, heads):
        picked = jnp.where(owner == head, full[head * BLOCK : (head + 1) * BLOCK], picked)
    return picked


def tile_bias(block, count, place_ref, base_ref, kind_ref, first_ref, end_ref):
    first = first_ref[pl.ds(block, 1), :]
    end = end_ref[pl.ds(block, 1), :]
    key = lax.broadcasted_iota(jnp.int32, (BLOCK, 2 * BLOCK), 0)
    starts = []
    biases = []
    for slot in range(count):
        starts.append(pl.multiple_of(place_ref[slot, block] * BLOCK, BLOCK))
        base = base_ref[slot, block]
        kind = kind_ref[slot, block]
        high = jnp.where(kind == 2, end, first + GLOBAL_BLOCKS * BLOCK)
        high = jnp.where(kind == 0, -1, high - base)
        allowed = (key >= first - base) & (key < high)
        biases.append(jnp.where(allowed, 0.0, masked_score))
    return starts, jnp.concatenate(biases, axis=0)


NT = (((1,), (1,)), ((), ()))
NN = (((1,), (0,)), ((), ()))
TN = (((0,), (0,)), ((), ()))


def gathered(pool_ref, starts, low, span):
    return jnp.concatenate(
        [pool_ref[pl.ds(start, BLOCK), low : low + span] for start in starts], axis=0
    )


def masked_scores(keys, query_diag, bias, heads):
    scores = lax.dot_general(keys, query_diag, NT, preferred_element_type=jnp.float32)
    return scores + jnp.concatenate([bias] * (heads // 2), axis=1)


def soft_columns(scores):
    top = jnp.max(scores, axis=0, keepdims=True)
    raised = jnp.exp(scores - top)
    total = jnp.sum(raised, axis=0, keepdims=True)
    return raised * (1.0 / total)


def load_pool(chunks, pool_ref, sems):
    rows = chunks[0].shape[0]
    copies = [
        pltpu.make_async_copy(chunk, pool_ref.at[pl.ds(n * rows, rows)], sems.at[n])
        for n, chunk in enumerate(chunks)
    ]
    for copy in copies:
        copy.start()
    return copies


def each_block(blocks, few, slots, count_ref, work):
    together = 2

    def step(n, carry):
        first = n * together
        short = count_ref[0, first] <= few
        for more in range(1, together):
            short = jnp.logical_and(short, count_ref[0, first + more] <= few)

        @pl.when(short)
        def _():
            work([first + more for more in range(together)], few)

        @pl.when(jnp.logical_not(short))
        def _():
            def single(more, carry):
                work([first + more], slots)
                return carry

            lax.fori_loop(0, together, single, 0)

        return carry

    lax.fori_loop(0, blocks // together, step, 0)


def split_store(source, kept, given, sems):
    rows = kept.shape[0]
    copies = [
        pltpu.make_async_copy(source.at[pl.ds(n * rows, rows)], target, sems.at[n])
        for n, target in enumerate((kept, given))
    ]
    for copy in copies:
        copy.start()
    for copy in copies:
        copy.wait()


def attend_kernel(sizes, *refs):
    blocks, slots, few, groups, width = sizes
    place_ref, base_ref, kind_ref, count_ref, first_ref, end_ref, query_ref = refs[:7]
    chunks = refs[7:-5]
    kept_ref, given_ref, out_ref, pool_ref, sems = refs[-5:]
    for copy in load_pool(chunks, pool_ref, sems):
        copy.wait()

    def work(chosen, count):
        tasks = []
        for block in chosen:
            starts, bias = tile_bias(
                block, count, place_ref, base_ref, kind_ref, first_ref, end_ref
            )
            here = pl.ds(pl.multiple_of(block * BLOCK, BLOCK), BLOCK)
            tasks += [(starts, bias, here, low, heads) for low, heads in groups]
        scores = []
        for starts, bias, here, low, heads in tasks:
            span = heads * HEAD_DIM
            query_diag = head_diag(query_ref[here, low : low + span], heads)
            keys = gathered(pool_ref, starts, low, span)
            scores.append(masked_scores(keys, query_diag, bias, heads))
        probs = [soft_columns(score).astype(jnp.bfloat16) for score in scores]
        for (starts, bias, here, low, heads), prob in zip(tasks, probs):
            span = heads * HEAD_DIM
            values = gathered(pool_ref, starts, width + low, span)
            mixed = lax.dot_general(prob, values, TN, preferred_element_type=jnp.float32)
            out_ref[here, low : low + span] = diag_rows(mixed, heads).astype(jnp.bfloat16)

    each_block(blocks, few, slots, count_ref, work)
    split_store(out_ref, kept_ref, given_ref, sems)


def attend_back_kernel(sizes, *refs):
    blocks, slots, few, groups, width, parts = sizes
    place_ref, base_ref, kind_ref, count_ref, first_ref, end_ref, query_ref = refs[:7]
    grad_parts = refs[7:9]
    chunks = refs[9 : 9 + parts]
    query_grads = refs[9 + parts : 11 + parts]
    outs = refs[11 + parts : 11 + 2 * parts]
    grad_ref, query_grad_ref, pool_ref, total_ref, sems = refs[11 + 2 * parts :]
    copies = load_pool(chunks, pool_ref, sems)
    rows = chunks[0].shape[0]
    for n, part in enumerate(grad_parts):
        copies.append(
            pltpu.make_async_copy(part, grad_ref.at[pl.ds(n * rows, rows)], sems.at[parts + n])
        )
        copies[-1].start()
    strip = 128

    def clear(n, carry):
        at = pl.ds(pl.multiple_of(n * strip, strip), strip)
        total_ref[at, :] = jnp.zeros((strip, 2 * width), jnp.float32)
        return carry

    lax.fori_loop(0, parts * rows // strip, clear, 0)
    for copy in copies:
        copy.wait()

    def work(chosen, count):
        tasks = []
        for block in chosen:
            starts, bias = tile_bias(
                block, count, place_ref, base_ref, kind_ref, first_ref, end_ref
            )
            here = pl.ds(pl.multiple_of(block * BLOCK, BLOCK), BLOCK)
            tasks += [(starts, bias, here, low, heads) for low, heads in groups]
        fronts = []
        for starts, bias, here, low, heads in tasks:
            span = heads * HEAD_DIM
            query_diag = head_diag(query_ref[here, low : low + span], heads)
            grad_diag = head_diag(grad_ref[here, low : low + span], heads)
            keys = gathered(pool_ref, starts, low, span)
            values = gathered(pool_ref, starts, width + low, span)
            scores = masked_scores(keys, query_diag, bias, heads)
            grad_probs = lax.dot_general(values, grad_diag, NT, preferred_element_type=jnp.float32)
            fronts.append((query_diag, grad_diag, keys, scores, grad_probs))
        for (starts, bias, here, low, heads), front in zip(tasks, fronts):
            query_diag, grad_diag, keys, scores, grad_probs = front
            span = heads * HEAD_DIM
            probs = soft_columns(scores)
            inner = jnp.sum(probs * grad_probs, axis=0, keepdims=True)
            grad_scores = (probs * (grad_probs - inner)).astype(jnp.bfloat16)
            grad_values = lax.dot_general(
                probs.astype(jnp.bfloat16), grad_diag, NN, preferred_element_type=jnp.float32
            )
            grad_keys = lax.dot_general(
                grad_scores, query_diag, NN, preferred_element_type=jnp.float32
            )
            grad_query = lax.dot_general(grad_scores, keys, TN, preferred_element_type=jnp.float32)
            query_grad_ref[here, low : low + span] = (
                diag_rows(grad_query, heads) * HEAD_DIM**-0.5
            ).astype(jnp.bfloat16)
            for slot, start in enumerate(starts):
                lines = slice(slot * BLOCK, (slot + 1) * BLOCK)
                total_ref[pl.ds(start, BLOCK), low : low + span] += grad_keys[lines]
                total_ref[pl.ds(start, BLOCK), width + low : width + low + span] += grad_values[
                    lines
                ]

    each_block(blocks, few, slots, count_ref, work)

    def lower(n, carry):
        at = pl.ds(pl.multiple_of(n * strip, strip), strip)
        pool_ref[at, :] = total_ref[at, :].astype(jnp.bfloat16)
        return carry

    split_store(query_grad_ref, *query_grads, sems)
    sends = []
    for n, out in enumerate(outs):
        lax.fori_loop(n * rows // strip, (n + 1) * rows // strip, lower, 0)
        send = pltpu.make_async_copy(pool_ref.at[pl.ds(n * rows, rows)], out, sems.at[n])
        send.start()
        sends.append(send)
    for send in sends:
        send.wait()


def attend(lists, query_rows, chunks, groups, slots, few):
    tokens, width = query_rows.shape
    rows = chunks[0].shape[0]
    parts = len(chunks)
    blocks = tokens // BLOCK
    smem = pl.BlockSpec(memory_space=pltpu.SMEM)
    vmem = pl.BlockSpec(memory_space=pltpu.VMEM)
    hbm = pl.BlockSpec(memory_space=pl.ANY)
    keys = few * BLOCK
    return pl.pallas_call(
        functools.partial(attend_kernel, (blocks, slots, few, groups, width)),
        out_shape=[jax.ShapeDtypeStruct((rows, width), jnp.bfloat16)] * 2,
        in_specs=[smem] * 4 + [vmem] * 3 + [hbm] * parts,
        out_specs=[hbm] * 2,
        scratch_shapes=[
            pltpu.VMEM((tokens, width), jnp.bfloat16),
            pltpu.VMEM((parts * rows, 2 * width), jnp.bfloat16),
            pltpu.SemaphoreType.DMA((parts,)),
        ],
        compiler_params=pltpu.CompilerParams(vmem_limit_bytes=VMEM_BYTES),
        cost_estimate=pl.CostEstimate(
            flops=16 * tokens * keys * width,
            bytes_accessed=4 * parts * rows * width,
            transcendentals=tokens * keys * width // HEAD_DIM,
        ),
        name="attend",
    )(*lists, query_rows, *chunks)


def attend_back(lists, query_rows, grad_parts, chunks, groups, slots, few):
    tokens, width = query_rows.shape
    rows = chunks[0].shape[0]
    parts = len(chunks)
    blocks = tokens // BLOCK
    smem = pl.BlockSpec(memory_space=pltpu.SMEM)
    vmem = pl.BlockSpec(memory_space=pltpu.VMEM)
    hbm = pl.BlockSpec(memory_space=pl.ANY)
    keys = few * BLOCK
    return pl.pallas_call(
        functools.partial(attend_back_kernel, (blocks, slots, few, groups, width, parts)),
        out_shape=[jax.ShapeDtypeStruct((rows, width), jnp.bfloat16)] * 2
        + [jax.ShapeDtypeStruct((rows, 2 * width), jnp.bfloat16)] * parts,
        in_specs=[smem] * 4 + [vmem] * 3 + [hbm] * (2 + parts),
        out_specs=[hbm] * (2 + parts),
        scratch_shapes=[
            pltpu.VMEM((tokens, width), jnp.bfloat16),
            pltpu.VMEM((tokens, width), jnp.bfloat16),
            pltpu.VMEM((parts * rows, 2 * width), jnp.bfloat16),
            pltpu.VMEM((parts * rows, 2 * width), jnp.float32),
            pltpu.SemaphoreType.DMA((parts + 2,)),
        ],
        compiler_params=pltpu.CompilerParams(vmem_limit_bytes=VMEM_BYTES),
        cost_estimate=pl.CostEstimate(
            flops=40 * tokens * keys * width,
            bytes_accessed=8 * parts * rows * width,
            transcendentals=tokens * keys * width // HEAD_DIM,
        ),
        name="attend_back",
    )(*lists, query_rows, *grad_parts, *chunks)


def row_norm(wide):
    mean = jnp.mean(wide, axis=-1, keepdims=True)
    centred = wide - mean
    inverse = lax.rsqrt(jnp.mean(centred * centred, axis=-1, keepdims=True) + layer_eps)
    return centred * inverse, inverse


def row_norm_back(grad, normal, inverse):
    mean = jnp.mean(grad, axis=-1, keepdims=True)
    along = jnp.mean(grad * normal, axis=-1, keepdims=True)
    return inverse * (grad - mean - normal * along)


def normal_parts(wide):
    size = jnp.abs(wide)
    bell = jnp.exp(-0.5 * wide * wide)
    step = 1.0 / (1.0 + (0.3275911 * math.sqrt(0.5)) * size)
    poly = 0.5 * 1.061405429
    for factor in (-1.453152027, 1.421413741, -0.284496736, 0.254829592):
        poly = poly * step + 0.5 * factor
    tail = poly * step * bell
    return jnp.where(wide < 0, tail, 1.0 - tail), bell * (1.0 / math.sqrt(2 * math.pi))


def column_sum(wide):
    return jnp.sum(wide, axis=0, keepdims=True)


def dense_kernel(sizes, *refs):
    tile, piece = sizes
    spot_ref, kept_ref, given_ref, input_ref, top_ref, vector_ref, offset_ref = refs[:7]
    weights = refs[7]
    out_ref, first_ref, grad_kept_ref, grad_given_ref, line_ref, hidden_line_ref = refs[8:14]
    grads = refs[14]
    expand_ref, mixer_ref, shrink_ref = refs[15:18]
    active_ref, pre_grad_ref, slope_ref = refs[18:21]
    middle_ref, ffn_ref, branch_ref, sems = refs[21:]
    bf16 = jnp.bfloat16
    f32 = jnp.float32
    tokens, width = input_ref.shape
    half = width // 2
    hidden = expand_ref.shape[1]
    core = spot_ref[1]
    fold = hidden // width

    def dot(left, right, kind):
        return lax.dot_general(left, right, kind, preferred_element_type=f32)

    places = [(mixer_ref, hidden, width), (expand_ref, 0, hidden)]
    for block in range(fold):
        part = shrink_ref.at[pl.ds(block * width, width)]
        places.append((part, hidden + (1 + block) * width, width))
    loads = [
        pltpu.make_async_copy(weights.at[:, pl.ds(low, span)], part, sems.at[n])
        for n, (part, low, span) in enumerate(places)
    ]
    for load in loads:
        load.start()
    loads[0].wait()

    line_ref[...] = jnp.zeros_like(line_ref)
    hidden_line_ref[...] = jnp.zeros_like(hidden_line_ref)
    vector = [vector_ref[pl.ds(n, 1), :] for n in range(8)]
    _, _, mixer_bias, first_gain, first_shift, shrink_bias, second_gain, second_shift = vector
    kept_rows = pl.ds(pl.multiple_of(core * half, half), half)
    given_rows = pl.ds(pl.multiple_of((1 - core) * half, half), half)

    def step(n, carry):
        at = pl.ds(pl.multiple_of(n * tile, tile), tile)
        first_sum = input_ref[at, :].astype(f32) + (
            dot(kept_ref[at, :], mixer_ref[kept_rows, :], NN)
            + dot(given_ref[at, :], mixer_ref[given_rows, :], NN)
            + mixer_bias
        )
        first_normal, first_inverse = row_norm(first_sum)
        middle = first_normal * first_gain + first_shift
        middle_low = middle.astype(bf16)
        middle_ref[at, :] = middle_low

        @pl.when(n == 0)
        def _():
            for load in loads[1:]:
                load.wait()

        second_sum = middle + shrink_bias
        for low in range(0, hidden, piece):
            span = slice(low, low + piece)
            pre = dot(middle_low, expand_ref[:, span], NN) + offset_ref[:, span]
            share, density = normal_parts(pre)
            active = (pre * share).astype(bf16)
            active_ref[at, span] = active
            slope_ref[:, span] = share + pre * density
            second_sum = second_sum + dot(active, shrink_ref[span, :], NN)
        second_normal, second_inverse = row_norm(second_sum)
        out_ref[at, :] = (second_normal * second_gain + second_shift).astype(bf16)
        top = top_ref[at, :].astype(f32)
        second = row_norm_back(top * second_gain, second_normal, second_inverse)
        ffn = second.astype(bf16)
        ffn_ref[at, :] = ffn
        middle_grad = second
        for low in range(0, hidden, piece):
            span = slice(low, low + piece)
            pre_grad = dot(ffn, shrink_ref[span, :], NT) * slope_ref[:, span]
            pre_low = pre_grad.astype(bf16)
            pre_grad_ref[at, span] = pre_low
            hidden_line_ref[:, span] += column_sum(pre_low.astype(f32))
            middle_grad = middle_grad + dot(pre_low, expand_ref[:, span], NT)
        first = row_norm_back(middle_grad * first_gain, first_normal, first_inverse)
        first_ref[at, :] = first
        branch = first.astype(bf16)
        branch_ref[at, :] = branch
        grad_kept_ref[at, :] = dot(branch, mixer_ref[kept_rows, :], NT).astype(bf16)
        grad_given_ref[at, :] = dot(branch, mixer_ref[given_rows, :], NT).astype(bf16)
        sums = [
            column_sum(branch.astype(f32)),
            column_sum(middle_grad * first_normal),
            column_sum(middle_grad),
            column_sum(ffn.astype(f32)),
            column_sum(top * second_normal),
            column_sum(top),
        ]
        for line, row in enumerate(sums):
            line_ref[pl.ds(2 + line, 1), :] += row
        return carry

    lax.fori_loop(0, tokens // tile, step, 0)

    stores = []

    def leave(slot):
        part, low, span = places[slot]
        stores.append(pltpu.make_async_copy(part, grads.at[:, pl.ds(low, span)], sems.at[slot]))
        stores[-1].start()

    strip = 768

    def shrink_step(n, carry):
        span = pl.ds(pl.multiple_of(n * strip, strip), strip)
        shrink_ref[span, :] = dot(active_ref[:, span], ffn_ref[...], TN).astype(bf16)
        return carry

    lax.fori_loop(0, hidden // strip, shrink_step, 0)
    for block in range(fold):
        leave(2 + block)
    for row in range(0, width, strip):
        rows = slice(row, row + strip)

        def expand_step(n, carry):
            span = pl.ds(pl.multiple_of(n * 2 * strip, 2 * strip), 2 * strip)
            expand_ref[rows, span] = dot(middle_ref[:, rows], pre_grad_ref[:, span], TN).astype(bf16)
            return carry

        lax.fori_loop(0, hidden // (2 * strip), expand_step, 0)
    leave(1)
    mixer_ref[kept_rows, :] = dot(kept_ref[...], branch_ref[...], TN).astype(bf16)
    mixer_ref[given_rows, :] = dot(given_ref[...], branch_ref[...], TN).astype(bf16)
    leave(0)
    for store in stores:
        store.wait()


def dense(spot, kept, given, inputs, top, vector_rows, hidden_offset, weights):
    tokens, width = inputs.shape
    hidden = hidden_offset.shape[1]
    fold = hidden // width
    tile = 512
    piece = 768
    bf16 = jnp.bfloat16
    f32 = jnp.float32
    smem = pl.BlockSpec(memory_space=pltpu.SMEM)
    vmem = pl.BlockSpec(memory_space=pltpu.VMEM)
    hbm = pl.BlockSpec(memory_space=pl.ANY)
    shape = jax.ShapeDtypeStruct
    return pl.pallas_call(
        functools.partial(dense_kernel, (tile, piece)),
        out_shape=[
            shape((tokens, width), bf16),
            shape((tokens, width), f32),
            shape((tokens, width // 2), bf16),
            shape((tokens, width // 2), bf16),
            shape((8, width), f32),
            shape((1, hidden), f32),
            shape(weights.shape, bf16),
        ],
        in_specs=[smem] + [vmem] * 6 + [hbm],
        out_specs=[vmem] * 6 + [hbm],
        scratch_shapes=[
            pltpu.VMEM((width, hidden), bf16),
            pltpu.VMEM((width, width), bf16),
            pltpu.VMEM((hidden, width), bf16),
            pltpu.VMEM((tokens, hidden), bf16),
            pltpu.VMEM((tokens, hidden), bf16),
            pltpu.VMEM((tile, hidden), f32),
            pltpu.VMEM((tokens, width), bf16),
            pltpu.VMEM((tokens, width), bf16),
            pltpu.VMEM((tokens, width), bf16),
            pltpu.SemaphoreType.DMA((2 + fold,)),
        ],
        compiler_params=pltpu.CompilerParams(vmem_limit_bytes=VMEM_BYTES),
        cost_estimate=pl.CostEstimate(
            flops=6 * tokens * width * (2 * hidden + width),
            bytes_accessed=8 * width * (2 * hidden + width),
            transcendentals=2 * tokens * hidden,
        ),
        name="dense",
    )(spot, kept, given, inputs, top, vector_rows, hidden_offset, weights)


def table_kernel(sizes, *refs):
    counts, half, line_count = sizes
    chunks = len(counts)
    spot_ref = refs[0]
    pieces = refs[1 : 1 + sum(counts)]
    refs = refs[1 + sum(counts) :]
    pair_grads = refs[:chunks]
    query_grads = refs[chunks : chunks + 2]
    dense_ref, hidden_ref = refs[chunks + 2 : chunks + 4]
    out_ref, total_ref, line_ref, rows_ref, grads_ref, query_ref, sems = refs[chunks + 4 :]
    core = spot_ref[1]
    width = rows_ref.shape[2]
    f32 = jnp.float32

    def fetch(n):
        slot = n % 2
        copies = []
        low = 0
        for piece in pieces[sum(counts[:n]) : sum(counts[: n + 1])]:
            target = rows_ref.at[slot, pl.ds(low, piece.shape[0])]
            copies.append(pltpu.make_async_copy(piece, target, sems.at[slot, len(copies)]))
            low += piece.shape[0]
        copies.append(pltpu.make_async_copy(pair_grads[n], grads_ref.at[slot], sems.at[slot, 2]))
        if n < 2:
            copies.append(
                pltpu.make_async_copy(query_grads[n], query_ref.at[slot], sems.at[slot, 3])
            )
        for copy in copies:
            copy.start()
        return copies

    line_ref[...] = jnp.zeros_like(line_ref)
    waiting = fetch(0)
    step = 384
    for n in range(chunks):
        following = fetch(n + 1) if n + 1 < chunks else []
        for copy in waiting:
            copy.wait()
        slot = n % 2
        for row in range(0, width, step):
            rows = rows_ref[slot, :, row : row + step]
            here = slice(row, row + step)
            for column in range(0, 2 * half, step):
                there = slice(column, column + step)
                part = lax.dot_general(
                    rows, grads_ref[slot, :, there], TN, preferred_element_type=f32
                )
                total_ref[here, there] = part if n == 0 else total_ref[here, there] + part
            if n < 2:
                there = slice(2 * half, 3 * half)
                part = lax.dot_general(rows, query_ref[slot], TN, preferred_element_type=f32)
                total_ref[here, there] = part if n == 0 else total_ref[here, there] + part
        line_ref[pl.ds(0, 1), :] += jnp.sum(
            grads_ref[slot, :, half:].astype(f32), axis=0, keepdims=True
        )
        if n < 2:
            line_ref[pl.ds(1, 1), :] += jnp.sum(
                query_ref[slot].astype(f32), axis=0, keepdims=True
            )
        waiting = following
    columns = 3 * half
    for row in range(0, width, step):
        out_ref[row : row + step, :columns] = total_ref[row : row + step, :].astype(jnp.bfloat16)
    low_core = lax.broadcasted_iota(jnp.int32, (8, width), 1) < half
    mine = low_core == (core == 0)
    halves = jnp.where(mine, jnp.concatenate([line_ref[...], line_ref[...]], axis=1), 0.0)
    vectors = [halves[1:2], halves[0:1], dense_ref[2:8, :]]
    for low in range(0, hidden_ref.shape[1], width):
        vectors.append(hidden_ref[:, low : low + width])
    wide = jnp.concatenate(vectors, axis=0)
    high = wide.astype(jnp.bfloat16).astype(f32)
    pad = jnp.zeros((128 - 2 * line_count, width), f32)
    packed = jnp.concatenate([high, wide - high, pad], axis=0)
    out_ref[:, columns:] = packed.T.astype(jnp.bfloat16)


def table_grads(spot, rows_in, pair_grads, query_grads, dense_lines, hidden_line):
    smem = pl.BlockSpec(memory_space=pltpu.SMEM)
    vmem = pl.BlockSpec(memory_space=pltpu.VMEM)
    hbm = pl.BlockSpec(memory_space=pl.ANY)
    counts = tuple(len(pieces) for pieces in rows_in)
    flat = [piece for pieces in rows_in for piece in pieces]
    rows, total = pair_grads[0].shape
    half = total // 2
    width = flat[0].shape[1]
    bf16 = jnp.bfloat16
    shape = jax.ShapeDtypeStruct
    return pl.pallas_call(
        functools.partial(table_kernel, (counts, half, 8 + hidden_line.shape[1] // width)),
        out_shape=shape((width, 3 * half + 128), bf16),
        in_specs=[smem] + [hbm] * (len(flat) + len(pair_grads) + 2) + [vmem] * 2,
        out_specs=vmem,
        scratch_shapes=[
            pltpu.VMEM((width, 3 * half), jnp.float32),
            pltpu.VMEM((8, half), jnp.float32),
            pltpu.VMEM((2, rows, width), bf16),
            pltpu.VMEM((2, rows, total), bf16),
            pltpu.VMEM((2, rows, half), bf16),
            pltpu.SemaphoreType.DMA((2, 4)),
        ],
        compiler_params=pltpu.CompilerParams(vmem_limit_bytes=VMEM_BYTES),
        cost_estimate=pl.CostEstimate(flops=10**10, bytes_accessed=4 * 10**7, transcendentals=0),
        name="table_grads",
    )(spot, *flat, *pair_grads, *query_grads, dense_lines, hidden_line)


def pick(flag, first, second):
    return jnp.where(flag == 0, first, second)


def split_low(wide, width):
    high = lax.reduce_precision(wide, 8, 7)
    parts = [high.astype(jnp.bfloat16), (wide - high).astype(jnp.bfloat16)]
    pad = width - 2 * wide.shape[-1]
    parts.append(jnp.zeros(wide.shape[:-1] + (pad,), jnp.bfloat16))
    return jnp.concatenate(parts, axis=-1)


def join_low(packed, count):
    wide = packed.astype(jnp.float32)
    return wide[..., :count] + wide[..., count : 2 * count]


def body(
    tokens_in,
    query_weight,
    query_bias,
    key_weight,
    value_weight,
    value_bias,
    mixer_weight,
    mixer_bias,
    first_gain,
    first_shift,
    expand_weight,
    expand_bias,
    shrink_weight,
    shrink_bias,
    second_gain,
    second_shift,
    doc_starts,
    random_blocks,
    cotangent,
):
    f32 = jnp.float32
    bf16 = jnp.bfloat16
    axes = ("head", "blk")
    head_count = lax.axis_size("head")
    cycle_size = lax.axis_size("blk")
    devices = head_count * cycle_size
    head_index = lax.axis_index("head")
    cycle_index = lax.axis_index("blk")
    side = head_index // 2
    core = head_index % 2
    level = cycle_index // 2
    turn = cycle_index % 2
    levels = cycle_size // 2
    local_rows = tokens_in.shape[1]
    model_width = tokens_in.shape[2]
    half_width = model_width // 2
    hidden = expand_weight.shape[1]
    fold = hidden // model_width
    own_rows = query_weight.shape[0]
    part_blocks = local_rows // BLOCK
    half_blocks = 2 * part_blocks
    total_blocks = part_blocks * devices
    slots = 3 + random_blocks.shape[1] + 2 * (GLOBAL_BLOCKS + 1)
    few = slots - GLOBAL_BLOCKS - 1
    groups = ((0, 4), (4 * HEAD_DIM, 2))

    def flat(head, cycle):
        return head * cycle_size + cycle

    everywhere = [(h, b) for h in range(head_count) for b in range(cycle_size)]
    over_side = [(flat(h, b), flat(h ^ 2, b)) for h, b in everywhere]
    over_core = [(flat(h, b), flat(h ^ 1, b)) for h, b in everywhere]
    over_turn = [(flat(h, b), flat(h, b ^ 1)) for h, b in everywhere]
    inward = [
        (flat(h, b), flat(h, b + (1 if h >= 2 else -1)))
        for h, b in everywhere
        if 0 <= b + (1 if h >= 2 else -1) < cycle_size
    ]
    outward = [
        (flat(h, b), flat(h, b + (-1 if h >= 2 else 1)))
        for h, b in everywhere
        if 0 <= b + (-1 if h >= 2 else 1) < cycle_size
    ]

    def send(array, pairs):
        return lax.ppermute(array, axes, pairs)

    def send_back(array, pairs):
        return lax.ppermute(array, axes, [(b, a) for a, b in pairs])

    together = lax.optimization_barrier

    half_index = 2 * cycle_index + side
    spot = jnp.stack([side, core, half_index]).astype(jnp.int32)

    vectors = [
        query_bias,
        value_bias,
        mixer_bias,
        first_gain,
        first_shift,
        shrink_bias,
        second_gain,
        second_shift,
    ]
    line_count = len(vectors) + fold
    line_width = 128
    per_row = -(-(len(vectors) + 1) // own_rows)
    gap = line_width // per_row
    shard = pack(
        key_weight, value_weight, query_weight, vectors + [expand_bias], per_row, gap
    )
    trio = 3 * half_width
    wide_columns = hidden + model_width
    rest_shard = jnp.concatenate(
        [
            expand_weight.reshape(own_rows, model_width, fold)
            .transpose(0, 2, 1)
            .reshape(own_rows, hidden),
            mixer_weight,
            shrink_weight.reshape(own_rows, hidden),
        ],
        axis=1,
    ).astype(bf16)

    latest = []

    def turn_for(array):
        return together((array, latest[-1]))[0] if latest else array

    def mark(array):
        latest.append(array)
        return array

    def done(array):
        return mark(turn_for(array))

    inputs = tokens_in[0]
    beside = send(inputs, over_side)
    near = send(inputs, inward)
    tables = lax.all_gather(shard, axes, axis=0, tiled=True)
    rest = lax.all_gather(together((rest_shard, shard))[0], axes, axis=0, tiled=True)
    inputs_other = send(inputs, over_core)
    inputs_other = done(inputs_other)
    near = done(near)
    passed = send(near, over_side)
    far = send(together((inputs, near))[0], outward)
    beside = done(beside)
    near_other = send(near, over_core)
    near_other = done(near_other)
    beside_other = send(together((beside, near_other))[0], over_core)
    beside_other = done(beside_other)
    tables = done(tables)
    table = jnp.concatenate(
        [pick(core, tables[:, :trio], tables[:, trio : 2 * trio]), tables[:, 2 * trio :]], axis=1
    )

    pair_matrix = table[:, :model_width]
    query_matrix = table[:, model_width:trio]
    every_line = table[:, trio:].astype(f32).reshape(devices, own_rows, line_width)

    def line_of(n, size):
        low = n % per_row * gap
        return every_line[:, n // per_row, low : low + size].reshape(devices * size)

    vector_rows = jnp.stack([line_of(n, own_rows) for n in range(len(vectors))])
    expand_offset = line_of(len(vectors), own_rows * fold)
    expand_offset = expand_offset.reshape(model_width, fold).T.reshape(1, hidden)
    query_offset = pick(core, vector_rows[0, :half_width], vector_rows[0, half_width:])
    value_offset = pick(core, vector_rows[1, :half_width], vector_rows[1, half_width:])
    pair_offset = jnp.concatenate([jnp.zeros((half_width,), f32), value_offset])
    picks = jnp.concatenate(
        [
            lax.dynamic_slice_in_dim(random_blocks, head_index * part_blocks, part_blocks),
            lax.dynamic_slice_in_dim(random_blocks, (head_index ^ 1) * part_blocks, part_blocks),
        ],
        axis=0,
    ).T
    picks = jnp.pad(picks, ((0, 0), (0, 2 * BLOCK - half_blocks)))
    lists = key_lists(
        spot, doc_starts, picks, part_blocks, total_blocks, slots, random_blocks.shape[1]
    )

    def project(rows, matrix, offset):
        return (jnp.dot(rows, matrix, preferred_element_type=f32) + offset).astype(bf16)

    def project_pair(rows):
        return project(rows, pair_matrix, pair_offset)

    query_rows = jnp.concatenate(
        [project(turn_for(rows), query_matrix, query_offset) for rows in (inputs, inputs_other)],
        axis=0,
    ) * jnp.asarray(HEAD_DIM**-0.5, bf16)
    mark(query_rows)
    rows_in = [[inputs], [inputs_other], [beside], [beside_other], [near], [near_other]]
    chunks = [mark(project_pair(turn_for(rows))) for (rows,) in rows_in]
    passed = done(passed)
    passed_other = send(passed, over_core)
    far = done(far)
    far_other = send(far, over_core)
    chunks.append(mark(project_pair(turn_for(passed))))
    passed_other = done(passed_other)
    chunks.append(mark(project_pair(passed_other)))
    chunks.append(mark(project_pair(turn_for(far))))
    far_other = done(far_other)
    chunks.append(mark(project_pair(far_other)))
    rows_in += [[passed], [passed_other], [far], [far_other]]
    mixed_kept, mixed_leaving = attend(lists, query_rows, chunks, groups, slots, few)
    mark(mixed_leaving)
    mixed_given = send(mixed_leaving, over_core)
    (
        layer_out,
        grad_first,
        grad_kept,
        grad_leaving,
        dense_lines,
        hidden_line,
        rest_grad,
    ) = dense(
        spot,
        mixed_kept,
        mixed_given,
        inputs,
        cotangent[0],
        vector_rows,
        expand_offset,
        rest,
    )
    mark(grad_leaving)
    grad_given = send(grad_leaving, over_core)
    rest_total = lax.psum_scatter(rest_grad, axes, scatter_dimension=0, tiled=True)
    pair_grads = attend_back(
        lists, query_rows, (grad_kept, grad_given), chunks, groups, slots, few
    )
    query_grads = pair_grads[:2]
    pair_grads = pair_grads[2:]

    mark(query_grads[0])

    def back(grad, matrix):
        return jnp.einsum("te,de->td", turn_for(grad), matrix, preferred_element_type=f32)

    def leave(n):
        total = back(pair_grads[2 * n + 1], pair_matrix)
        if n == 0:
            total = total + back(query_grads[1], query_matrix)
        return send(mark(total.astype(bf16)), over_core)

    def stay(n, *extras):
        total = back(pair_grads[2 * n], pair_matrix)
        for extra in extras:
            total = total + extra.astype(f32)
        return mark(total.astype(bf16))

    passed_given = leave(3)
    far_given = leave(4)
    passed_given = done(passed_given)
    passed_back = send(stay(3, passed_given), over_side)
    near_given = leave(2)
    far_given = done(far_given)
    far_back = send_back(stay(4, far_given), outward)
    near_given = done(near_given)
    beside_given = leave(1)
    own_given = leave(0)
    table_grad = mark(
        table_grads(
            spot,
            rows_in,
            pair_grads,
            [turn_for(grad) for grad in query_grads],
            dense_lines,
            hidden_line,
        )
    )
    by_head = lax.all_to_all(
        table_grad.reshape(head_count, cycle_size * own_rows, trio + line_width),
        "head",
        split_axis=0,
        concat_axis=0,
        tiled=True,
    )
    beside_given = done(beside_given)
    own_given = done(own_given)
    passed_back = done(passed_back)
    far_back = done(far_back)
    near_back = send_back(stay(2, near_given, passed_back), inward)
    beside_back = send(stay(1, beside_given), over_side)
    by_head = done(by_head).reshape(2, 2, cycle_size, own_rows, trio + line_width)
    by_core = jnp.sum(by_head[..., :trio].astype(f32), axis=0).astype(bf16)
    line_sum = jnp.sum(join_low(by_head[..., trio:], line_count), axis=(0, 1))
    packed = mark(
        jnp.concatenate([by_core[0], by_core[1], split_low(line_sum, line_width)], axis=-1)
    )
    arrived = lax.all_to_all(packed, "blk", split_axis=0, concat_axis=0, tiled=True)
    own_total = mark(
        grad_first
        + back(pair_grads[0], pair_matrix)
        + back(query_grads[0], query_matrix)
        + own_given.astype(f32)
        + far_back.astype(f32)
    )
    near_back = done(near_back)
    arrived = done(arrived)
    table_own = jnp.sum(arrived[..., : 2 * trio].astype(f32), axis=0)
    line_own = jnp.sum(join_low(arrived[..., 2 * trio :], line_count), axis=0)
    rest_total = rest_total.astype(f32)
    input_grad = own_total + beside_back.astype(f32) + near_back.astype(f32)

    def columns_of(which):
        low = which * half_width
        return jnp.concatenate(
            [table_own[:, at : at + half_width] for at in (low, trio + low)], axis=1
        )

    return (
        layer_out[None],
        input_grad[None],
        columns_of(2),
        line_own[:, 0],
        columns_of(0),
        columns_of(1),
        line_own[:, 1],
        rest_total[:, hidden:wide_columns],
        line_own[:, 2],
        line_own[:, 3],
        line_own[:, 4],
        rest_total[:, :hidden]
        .reshape(own_rows, fold, model_width)
        .transpose(0, 2, 1)
        .reshape(own_rows, hidden),
        line_own[:, len(vectors) :].reshape(-1),
        rest_total[:, wide_columns:].reshape(own_rows * fold, model_width),
        line_own[:, 5],
        line_own[:, 6],
        line_own[:, 7],
    )


def solution(mesh):
    in_specs = (
        P("blk", "head", None),
        P(("head", "blk"), None),
        P(("head", "blk")),
        P(("head", "blk"), None),
        P(("head", "blk"), None),
        P(("head", "blk")),
        P(("head", "blk"), None),
        P(("head", "blk")),
        P(("head", "blk")),
        P(("head", "blk")),
        P(("head", "blk"), None),
        P(("head", "blk")),
        P(("head", "blk"), None),
        P(("head", "blk")),
        P(("head", "blk")),
        P(("head", "blk")),
        P(),
        P("blk", None),
        P("blk", "head", None),
    )
    out_specs = (
        P("blk", "head", None),
        P("blk", "head", None),
        P(("head", "blk"), None),
        P(("head", "blk")),
        P(("head", "blk"), None),
        P(("head", "blk"), None),
        P(("head", "blk")),
        P(("head", "blk"), None),
        P(("head", "blk")),
        P(("head", "blk")),
        P(("head", "blk")),
        P(("head", "blk"), None),
        P(("head", "blk")),
        P(("head", "blk"), None),
        P(("head", "blk")),
        P(("head", "blk")),
        P(("head", "blk")),
    )
    return jax.shard_map(body, mesh=mesh, in_specs=in_specs, out_specs=out_specs, check_vma=False)
```

```python
import functools
import math

import jax
import jax.numpy as jnp
from jax import lax
from jax.experimental import pallas as pl
from jax.experimental.pallas import tpu as pltpu
from jax.sharding import PartitionSpec as P

HEADS = 12
HEAD_DIM = 64
BLOCK = 64
GLOBAL_BLOCKS = 2
MAXDOC = 4096
VMEM_BYTES = 60 * 2**20

layer_eps = 1e-12
masked_score = -1e30

def pack_kernel(sizes, *refs):
    half, per_row, gap = sizes
    key_ref, value_ref, query_ref = refs[:3]
    vectors = refs[3:-1]
    out_ref = refs[-1]
    rows, total = out_ref.shape
    bf16 = jnp.bfloat16
    for n, source in enumerate((key_ref, value_ref, query_ref)):
        for core in range(2):
            at = (3 * core + n) * half
            out_ref[:, at : at + half] = source[:, core * half : (core + 1) * half].astype(bf16)
    line = lax.broadcasted_iota(jnp.int32, (rows, 128), 0)
    block = jnp.zeros((rows, 128), jnp.float32)
    for n, vector in enumerate(vectors):
        row = vector[...]
        low = n % per_row * gap
        pieces = [row, jnp.zeros((1, 128 - low - row.shape[1]), jnp.float32)]
        if low:
            pieces = [jnp.zeros((1, low), jnp.float32)] + pieces
        block = jnp.where(line == n // per_row, block + jnp.concatenate(pieces, axis=1), block)
    out_ref[:, 6 * half :] = block.astype(bf16)


def pack(key_weight, value_weight, query_weight, vectors, per_row, gap):
    rows, width = key_weight.shape
    vmem = pl.BlockSpec(memory_space=pltpu.VMEM)
    return pl.pallas_call(
        functools.partial(pack_kernel, (width // 2, per_row, gap)),
        out_shape=jax.ShapeDtypeStruct((rows, 3 * width + 128), jnp.bfloat16),
        in_specs=[vmem] * (3 + len(vectors)),
        out_specs=vmem,
        name="pack",
    )(key_weight, value_weight, query_weight, *[vector[None] for vector in vectors])


def list_kernel(sizes, spot_ref, starts_ref, picks_ref, *outs):
    place_ref, base_ref, kind_ref, count_ref, first_ref, end_ref = outs
    part_blocks, half_blocks, total_blocks, slots, random = sizes
    bits = BLOCK.bit_length() - 1
    part_bits = part_blocks.bit_length() - 1
    half_bits = half_blocks.bit_length() - 1
    lanes = 2 * BLOCK
    side, core, half_index = [spot_ref[n] for n in range(3)]
    docs = [starts_ref[n] for n in range(starts_ref.shape[0])]
    int32 = jnp.int32

    def block_of(n):
        part = jnp.where(n < part_blocks, core, 1 - core)
        return half_index * half_blocks + part * part_blocks + (n & (part_blocks - 1))

    def first_of(position):
        first = jnp.zeros(position.shape, int32)
        for start in docs:
            first = jnp.where(position >= start, start, first)
        return first

    def end_of(position):
        end = jnp.full(position.shape, total_blocks * BLOCK, int32)
        for start in docs[::-1]:
            end = jnp.where(position < start, start, end)
        return end

    rows = lax.broadcasted_iota(int32, (half_blocks, lanes), 0)
    columns = lax.broadcasted_iota(int32, (half_blocks, lanes), 1)
    positions = block_of(rows) * BLOCK + (columns & (BLOCK - 1))
    first_ref[...] = first_of(positions)
    end_ref[...] = end_of(positions)

    block = block_of(lax.broadcasted_iota(int32, (1, lanes), 1))
    lead = block * BLOCK
    first_lead = first_of(lead)
    first_tail = first_of(lead + BLOCK - 1)
    end_tail = end_of(lead + BLOCK - 1)
    picks = [picks_ref[pl.ds(n, 1), :] for n in range(random)]
    candidates = [block - 1, block, block + 1] + picks
    for anchor in (first_lead, first_tail):
        candidates += [(anchor >> bits) + offset for offset in range(GLOBAL_BLOCKS + 1)]
    candidates = [jnp.clip(candidate, 0, total_blocks - 1) for candidate in candidates]
    seated = [[jnp.zeros((1, lanes), int32)] * 3 for _ in range(slots)]
    rank = jnp.zeros((1, lanes), int32)
    for n, candidate in enumerate(candidates):
        useful = candidate >= 0
        for earlier in candidates[:n]:
            useful = useful & (candidate != earlier)
        nearby = jnp.abs(candidate - block) <= 1
        for chosen in picks:
            nearby = nearby | (candidate == chosen)
        base = candidate * BLOCK
        useful = useful & (base + BLOCK > first_lead) & (base < end_tail)
        useful = useful & (nearby | (base < first_tail + GLOBAL_BLOCKS * BLOCK))
        apart = (candidate >> half_bits) - half_index
        reach = jnp.abs(apart)
        useful = useful & (reach <= 2)
        later = (apart > 0).astype(int32)
        slot = jnp.where(later == 1 - side, reach, reach + 2)
        slot = jnp.where(reach == 0, 0, slot)
        part = ((candidate >> part_bits) & 1) ^ core
        place = (2 * slot + part) * part_blocks + (candidate & (part_blocks - 1))
        values = (place, base, 1 + nearby.astype(int32))
        for seat in range(n + 1):
            here = useful & (rank == seat)
            seated[seat] = [jnp.where(here, new, old) for new, old in zip(values, seated[seat])]
        rank = rank + useful.astype(int32)
    for seat in range(slots):
        for out, value in zip((place_ref, base_ref, kind_ref), seated[seat]):
            out[pl.ds(seat, 1), :] = value
    count_ref[...] = rank


def key_lists(spot, doc_starts, picks, part_blocks, total_blocks, slots, random):
    lanes = 2 * BLOCK
    half_blocks = 2 * part_blocks
    shape = jax.ShapeDtypeStruct
    smem = pl.BlockSpec(memory_space=pltpu.SMEM)
    vmem = pl.BlockSpec(memory_space=pltpu.VMEM)
    return pl.pallas_call(
        functools.partial(
            list_kernel, (part_blocks, half_blocks, total_blocks, slots, random)
        ),
        out_shape=[shape((slots, lanes), jnp.int32)] * 3
        + [shape((1, lanes), jnp.int32)]
        + [shape((half_blocks, lanes), jnp.int32)] * 2,
        in_specs=[smem, smem, vmem],
        out_specs=[vmem] * 6,
        name="key_lists",
    )(spot, doc_starts, picks)


def chunk_tile(rows, width):
    return lax.broadcasted_iota(jnp.int32, (rows, width), 1) // HEAD_DIM


def head_diag(tile, heads):
    owner = chunk_tile(BLOCK, heads * HEAD_DIM)
    return jnp.concatenate(
        [jnp.where(owner == head, tile, jnp.zeros_like(tile)) for head in range(heads)], axis=0
    )


def diag_rows(full, heads):
    owner = chunk_tile(BLOCK, heads * HEAD_DIM)
    picked = full[:BLOCK]
    for head in range(1, heads):
        picked = jnp.where(owner == head, full[head * BLOCK : (head + 1) * BLOCK], picked)
    return picked


def tile_bias(block, count, place_ref, base_ref, kind_ref, first_ref, end_ref):
    first = first_ref[pl.ds(block, 1), :]
    end = end_ref[pl.ds(block, 1), :]
    key = lax.broadcasted_iota(jnp.int32, (BLOCK, 2 * BLOCK), 0)
    starts = []
    biases = []
    for slot in range(count):
        starts.append(pl.multiple_of(place_ref[slot, block] * BLOCK, BLOCK))
        base = base_ref[slot, block]
        kind = kind_ref[slot, block]
        high = jnp.where(kind == 2, end, first + GLOBAL_BLOCKS * BLOCK)
        high = jnp.where(kind == 0, -1, high - base)
        allowed = (key >= first - base) & (key < high)
        biases.append(jnp.where(allowed, 0.0, masked_score))
    return starts, jnp.concatenate(biases, axis=0)


NT = (((1,), (1,)), ((), ()))
NN = (((1,), (0,)), ((), ()))
TN = (((0,), (0,)), ((), ()))


def gathered(pool_ref, starts, low, span):
    return jnp.concatenate(
        [pool_ref[pl.ds(start, BLOCK), low : low + span] for start in starts], axis=0
    )


def masked_scores(keys, query_diag, bias, heads):
    scores = lax.dot_general(keys, query_diag, NT, preferred_element_type=jnp.float32)
    return scores + jnp.concatenate([bias] * (heads // 2), axis=1)


def soft_columns(scores):
    top = jnp.max(scores, axis=0, keepdims=True)
    raised = jnp.exp(scores - top)
    total = jnp.sum(raised, axis=0, keepdims=True)
    return raised * (1.0 / total)


def load_pool(chunks, pool_ref, sems):
    rows = chunks[0].shape[0]
    copies = [
        pltpu.make_async_copy(chunk, pool_ref.at[pl.ds(n * rows, rows)], sems.at[n])
        for n, chunk in enumerate(chunks)
    ]
    for copy in copies:
        copy.start()
    return copies


def each_block(blocks, few, slots, count_ref, work):
    together = 2

    def step(n, carry):
        first = n * together
        short = count_ref[0, first] <= few
        for more in range(1, together):
            short = jnp.logical_and(short, count_ref[0, first + more] <= few)

        @pl.when(short)
        def _():
            work([first + more for more in range(together)], few)

        @pl.when(jnp.logical_not(short))
        def _():
            def single(more, carry):
                work([first + more], slots)
                return carry

            lax.fori_loop(0, together, single, 0)

        return carry

    lax.fori_loop(0, blocks // together, step, 0)


def split_store(source, kept, given, sems):
    rows = kept.shape[0]
    copies = [
        pltpu.make_async_copy(source.at[pl.ds(n * rows, rows)], target, sems.at[n])
        for n, target in enumerate((kept, given))
    ]
    for copy in copies:
        copy.start()
    for copy in copies:
        copy.wait()


def attend_kernel(sizes, *refs):
    blocks, slots, few, groups, width = sizes
    place_ref, base_ref, kind_ref, count_ref, first_ref, end_ref, query_ref = refs[:7]
    chunks = refs[7:-5]
    kept_ref, given_ref, out_ref, pool_ref, sems = refs[-5:]
    for copy in load_pool(chunks, pool_ref, sems):
        copy.wait()

    def work(chosen, count):
        tasks = []
        for block in chosen:
            starts, bias = tile_bias(
                block, count, place_ref, base_ref, kind_ref, first_ref, end_ref
            )
            here = pl.ds(pl.multiple_of(block * BLOCK, BLOCK), BLOCK)
            tasks += [(starts, bias, here, low, heads) for low, heads in groups]
        scores = []
        for starts, bias, here, low, heads in tasks:
            span = heads * HEAD_DIM
            query_diag = head_diag(query_ref[here, low : low + span], heads)
            keys = gathered(pool_ref, starts, low, span)
            scores.append(masked_scores(keys, query_diag, bias, heads))
        probs = [soft_columns(score).astype(jnp.bfloat16) for score in scores]
        for (starts, bias, here, low, heads), prob in zip(tasks, probs):
            span = heads * HEAD_DIM
            values = gathered(pool_ref, starts, width + low, span)
            mixed = lax.dot_general(prob, values, TN, preferred_element_type=jnp.float32)
            out_ref[here, low : low + span] = diag_rows(mixed, heads).astype(jnp.bfloat16)

    each_block(blocks, few, slots, count_ref, work)
    split_store(out_ref, kept_ref, given_ref, sems)


def attend_back_kernel(sizes, *refs):
    blocks, slots, few, groups, width, parts = sizes
    place_ref, base_ref, kind_ref, count_ref, first_ref, end_ref, query_ref = refs[:7]
    grad_parts = refs[7:9]
    chunks = refs[9 : 9 + parts]
    query_grads = refs[9 + parts : 11 + parts]
    outs = refs[11 + parts : 11 + 2 * parts]
    grad_ref, query_grad_ref, pool_ref, total_ref, sems = refs[11 + 2 * parts :]
    copies = load_pool(chunks, pool_ref, sems)
    rows = chunks[0].shape[0]
    for n, part in enumerate(grad_parts):
        copies.append(
            pltpu.make_async_copy(part, grad_ref.at[pl.ds(n * rows, rows)], sems.at[parts + n])
        )
        copies[-1].start()
    strip = 128

    def clear(n, carry):
        at = pl.ds(pl.multiple_of(n * strip, strip), strip)
        total_ref[at, :] = jnp.zeros((strip, 2 * width), jnp.float32)
        return carry

    lax.fori_loop(0, parts * rows // strip, clear, 0)
    for copy in copies:
        copy.wait()

    def work(chosen, count):
        tasks = []
        for block in chosen:
            starts, bias = tile_bias(
                block, count, place_ref, base_ref, kind_ref, first_ref, end_ref
            )
            here = pl.ds(pl.multiple_of(block * BLOCK, BLOCK), BLOCK)
            tasks += [(starts, bias, here, low, heads) for low, heads in groups]
        fronts = []
        for starts, bias, here, low, heads in tasks:
            span = heads * HEAD_DIM
            query_diag = head_diag(query_ref[here, low : low + span], heads)
            grad_diag = head_diag(grad_ref[here, low : low + span], heads)
            keys = gathered(pool_ref, starts, low, span)
            values = gathered(pool_ref, starts, width + low, span)
            scores = masked_scores(keys, query_diag, bias, heads)
            grad_probs = lax.dot_general(values, grad_diag, NT, preferred_element_type=jnp.float32)
            fronts.append((query_diag, grad_diag, keys, scores, grad_probs))
        for (starts, bias, here, low, heads), front in zip(tasks, fronts):
            query_diag, grad_diag, keys, scores, grad_probs = front
            span = heads * HEAD_DIM
            probs = soft_columns(scores)
            inner = jnp.sum(probs * grad_probs, axis=0, keepdims=True)
            grad_scores = (probs * (grad_probs - inner)).astype(jnp.bfloat16)
            grad_values = lax.dot_general(
                probs.astype(jnp.bfloat16), grad_diag, NN, preferred_element_type=jnp.float32
            )
            grad_keys = lax.dot_general(
                grad_scores, query_diag, NN, preferred_element_type=jnp.float32
            )
            grad_query = lax.dot_general(grad_scores, keys, TN, preferred_element_type=jnp.float32)
            query_grad_ref[here, low : low + span] = (
                diag_rows(grad_query, heads) * HEAD_DIM**-0.5
            ).astype(jnp.bfloat16)
            for slot, start in enumerate(starts):
                lines = slice(slot * BLOCK, (slot + 1) * BLOCK)
                total_ref[pl.ds(start, BLOCK), low : low + span] += grad_keys[lines]
                total_ref[pl.ds(start, BLOCK), width + low : width + low + span] += grad_values[
                    lines
                ]

    each_block(blocks, few, slots, count_ref, work)

    def lower(n, carry):
        at = pl.ds(pl.multiple_of(n * strip, strip), strip)
        pool_ref[at, :] = total_ref[at, :].astype(jnp.bfloat16)
        return carry

    split_store(query_grad_ref, *query_grads, sems)
    sends = []
    for n, out in enumerate(outs):
        lax.fori_loop(n * rows // strip, (n + 1) * rows // strip, lower, 0)
        send = pltpu.make_async_copy(pool_ref.at[pl.ds(n * rows, rows)], out, sems.at[n])
        send.start()
        sends.append(send)
    for send in sends:
        send.wait()


def attend(lists, query_rows, chunks, groups, slots, few):
    tokens, width = query_rows.shape
    rows = chunks[0].shape[0]
    parts = len(chunks)
    blocks = tokens // BLOCK
    smem = pl.BlockSpec(memory_space=pltpu.SMEM)
    vmem = pl.BlockSpec(memory_space=pltpu.VMEM)
    hbm = pl.BlockSpec(memory_space=pl.ANY)
    keys = few * BLOCK
    return pl.pallas_call(
        functools.partial(attend_kernel, (blocks, slots, few, groups, width)),
        out_shape=[jax.ShapeDtypeStruct((rows, width), jnp.bfloat16)] * 2,
        in_specs=[smem] * 4 + [vmem] * 3 + [hbm] * parts,
        out_specs=[hbm] * 2,
        scratch_shapes=[
            pltpu.VMEM((tokens, width), jnp.bfloat16),
            pltpu.VMEM((parts * rows, 2 * width), jnp.bfloat16),
            pltpu.SemaphoreType.DMA((parts,)),
        ],
        compiler_params=pltpu.CompilerParams(vmem_limit_bytes=VMEM_BYTES),
        cost_estimate=pl.CostEstimate(
            flops=16 * tokens * keys * width,
            bytes_accessed=4 * parts * rows * width,
            transcendentals=tokens * keys * width // HEAD_DIM,
        ),
        name="attend",
    )(*lists, query_rows, *chunks)


def attend_back(lists, query_rows, grad_parts, chunks, groups, slots, few):
    tokens, width = query_rows.shape
    rows = chunks[0].shape[0]
    parts = len(chunks)
    blocks = tokens // BLOCK
    smem = pl.BlockSpec(memory_space=pltpu.SMEM)
    vmem = pl.BlockSpec(memory_space=pltpu.VMEM)
    hbm = pl.BlockSpec(memory_space=pl.ANY)
    keys = few * BLOCK
    return pl.pallas_call(
        functools.partial(attend_back_kernel, (blocks, slots, few, groups, width, parts)),
        out_shape=[jax.ShapeDtypeStruct((rows, width), jnp.bfloat16)] * 2
        + [jax.ShapeDtypeStruct((rows, 2 * width), jnp.bfloat16)] * parts,
        in_specs=[smem] * 4 + [vmem] * 3 + [hbm] * (2 + parts),
        out_specs=[hbm] * (2 + parts),
        scratch_shapes=[
            pltpu.VMEM((tokens, width), jnp.bfloat16),
            pltpu.VMEM((tokens, width), jnp.bfloat16),
            pltpu.VMEM((parts * rows, 2 * width), jnp.bfloat16),
            pltpu.VMEM((parts * rows, 2 * width), jnp.float32),
            pltpu.SemaphoreType.DMA((parts + 2,)),
        ],
        compiler_params=pltpu.CompilerParams(vmem_limit_bytes=VMEM_BYTES),
        cost_estimate=pl.CostEstimate(
            flops=40 * tokens * keys * width,
            bytes_accessed=8 * parts * rows * width,
            transcendentals=tokens * keys * width // HEAD_DIM,
        ),
        name="attend_back",
    )(*lists, query_rows, *grad_parts, *chunks)


def row_norm(wide):
    mean = jnp.mean(wide, axis=-1, keepdims=True)
    centred = wide - mean
    inverse = lax.rsqrt(jnp.mean(centred * centred, axis=-1, keepdims=True) + layer_eps)
    return centred * inverse, inverse


def row_norm_back(grad, normal, inverse):
    mean = jnp.mean(grad, axis=-1, keepdims=True)
    along = jnp.mean(grad * normal, axis=-1, keepdims=True)
    return inverse * (grad - mean - normal * along)


def normal_parts(wide):
    size = jnp.abs(wide)
    bell = jnp.exp(-0.5 * wide * wide)
    step = 1.0 / (1.0 + (0.3275911 * math.sqrt(0.5)) * size)
    poly = 0.5 * 1.061405429
    for factor in (-1.453152027, 1.421413741, -0.284496736, 0.254829592):
        poly = poly * step + 0.5 * factor
    tail = poly * step * bell
    return jnp.where(wide < 0, tail, 1.0 - tail), bell * (1.0 / math.sqrt(2 * math.pi))


def column_sum(wide):
    return jnp.sum(wide, axis=0, keepdims=True)


def dense_kernel(sizes, *refs):
    tile, piece = sizes
    spot_ref, kept_ref, given_ref, input_ref, top_ref, vector_ref, offset_ref = refs[:7]
    weights = refs[7]
    out_ref, first_ref, grad_kept_ref, grad_given_ref, line_ref, hidden_line_ref = refs[8:14]
    grads = refs[14]
    expand_ref, mixer_ref, shrink_ref = refs[15:18]
    active_ref, pre_grad_ref, slope_ref = refs[18:21]
    middle_ref, ffn_ref, branch_ref, sems = refs[21:]
    bf16 = jnp.bfloat16
    f32 = jnp.float32
    tokens, width = input_ref.shape
    half = width // 2
    hidden = expand_ref.shape[1]
    core = spot_ref[1]
    fold = hidden // width

    def dot(left, right, kind):
        return lax.dot_general(left, right, kind, preferred_element_type=f32)

    places = [(mixer_ref, hidden, width), (expand_ref, 0, hidden)]
    for block in range(fold):
        part = shrink_ref.at[pl.ds(block * width, width)]
        places.append((part, hidden + (1 + block) * width, width))
    loads = [
        pltpu.make_async_copy(weights.at[:, pl.ds(low, span)], part, sems.at[n])
        for n, (part, low, span) in enumerate(places)
    ]
    for load in loads:
        load.start()
    loads[0].wait()

    line_ref[...] = jnp.zeros_like(line_ref)
    hidden_line_ref[...] = jnp.zeros_like(hidden_line_ref)
    vector = [vector_ref[pl.ds(n, 1), :] for n in range(8)]
    _, _, mixer_bias, first_gain, first_shift, shrink_bias, second_gain, second_shift = vector
    kept_rows = pl.ds(pl.multiple_of(core * half, half), half)
    given_rows = pl.ds(pl.multiple_of((1 - core) * half, half), half)

    def step(n, carry):
        at = pl.ds(pl.multiple_of(n * tile, tile), tile)
        first_sum = input_ref[at, :].astype(f32) + (
            dot(kept_ref[at, :], mixer_ref[kept_rows, :], NN)
            + dot(given_ref[at, :], mixer_ref[given_rows, :], NN)
            + mixer_bias
        )
        first_normal, first_inverse = row_norm(first_sum)
        middle = first_normal * first_gain + first_shift
        middle_low = middle.astype(bf16)
        middle_ref[at, :] = middle_low

        @pl.when(n == 0)
        def _():
            for load in loads[1:]:
                load.wait()

        second_sum = middle + shrink_bias
        for low in range(0, hidden, piece):
            span = slice(low, low + piece)
            pre = dot(middle_low, expand_ref[:, span], NN) + offset_ref[:, span]
            share, density = normal_parts(pre)
            active = (pre * share).astype(bf16)
            active_ref[at, span] = active
            slope_ref[:, span] = share + pre * density
            second_sum = second_sum + dot(active, shrink_ref[span, :], NN)
        second_normal, second_inverse = row_norm(second_sum)
        out_ref[at, :] = (second_normal * second_gain + second_shift).astype(bf16)
        top = top_ref[at, :].astype(f32)
        second = row_norm_back(top * second_gain, second_normal, second_inverse)
        ffn = second.astype(bf16)
        ffn_ref[at, :] = ffn
        middle_grad = second
        for low in range(0, hidden, piece):
            span = slice(low, low + piece)
            pre_grad = dot(ffn, shrink_ref[span, :], NT) * slope_ref[:, span]
            pre_low = pre_grad.astype(bf16)
            pre_grad_ref[at, span] = pre_low
            hidden_line_ref[:, span] += column_sum(pre_low.astype(f32))
            middle_grad = middle_grad + dot(pre_low, expand_ref[:, span], NT)
        first = row_norm_back(middle_grad * first_gain, first_normal, first_inverse)
        first_ref[at, :] = first
        branch = first.astype(bf16)
        branch_ref[at, :] = branch
        grad_kept_ref[at, :] = dot(branch, mixer_ref[kept_rows, :], NT).astype(bf16)
        grad_given_ref[at, :] = dot(branch, mixer_ref[given_rows, :], NT).astype(bf16)
        sums = [
            column_sum(branch.astype(f32)),
            column_sum(middle_grad * first_normal),
            column_sum(middle_grad),
            column_sum(ffn.astype(f32)),
            column_sum(top * second_normal),
            column_sum(top),
        ]
        for line, row in enumerate(sums):
            line_ref[pl.ds(2 + line, 1), :] += row
        return carry

    lax.fori_loop(0, tokens // tile, step, 0)

    stores = []

    def leave(slot):
        part, low, span = places[slot]
        stores.append(pltpu.make_async_copy(part, grads.at[:, pl.ds(low, span)], sems.at[slot]))
        stores[-1].start()

    strip = 768

    def shrink_step(n, carry):
        span = pl.ds(pl.multiple_of(n * strip, strip), strip)
        shrink_ref[span, :] = dot(active_ref[:, span], ffn_ref[...], TN).astype(bf16)
        return carry

    lax.fori_loop(0, hidden // strip, shrink_step, 0)
    for block in range(fold):
        leave(2 + block)
    for row in range(0, width, strip):
        rows = slice(row, row + strip)

        def expand_step(n, carry):
            span = pl.ds(pl.multiple_of(n * 2 * strip, 2 * strip), 2 * strip)
            expand_ref[rows, span] = dot(middle_ref[:, rows], pre_grad_ref[:, span], TN).astype(bf16)
            return carry

        lax.fori_loop(0, hidden // (2 * strip), expand_step, 0)
    leave(1)
    mixer_ref[kept_rows, :] = dot(kept_ref[...], branch_ref[...], TN).astype(bf16)
    mixer_ref[given_rows, :] = dot(given_ref[...], branch_ref[...], TN).astype(bf16)
    leave(0)
    for store in stores:
        store.wait()


def dense(spot, kept, given, inputs, top, vector_rows, hidden_offset, weights):
    tokens, width = inputs.shape
    hidden = hidden_offset.shape[1]
    fold = hidden // width
    tile = 512
    piece = 768
    bf16 = jnp.bfloat16
    f32 = jnp.float32
    smem = pl.BlockSpec(memory_space=pltpu.SMEM)
    vmem = pl.BlockSpec(memory_space=pltpu.VMEM)
    hbm = pl.BlockSpec(memory_space=pl.ANY)
    shape = jax.ShapeDtypeStruct
    return pl.pallas_call(
        functools.partial(dense_kernel, (tile, piece)),
        out_shape=[
            shape((tokens, width), bf16),
            shape((tokens, width), f32),
            shape((tokens, width // 2), bf16),
            shape((tokens, width // 2), bf16),
            shape((8, width), f32),
            shape((1, hidden), f32),
            shape(weights.shape, bf16),
        ],
        in_specs=[smem] + [vmem] * 6 + [hbm],
        out_specs=[vmem] * 6 + [hbm],
        scratch_shapes=[
            pltpu.VMEM((width, hidden), bf16),
            pltpu.VMEM((width, width), bf16),
            pltpu.VMEM((hidden, width), bf16),
            pltpu.VMEM((tokens, hidden), bf16),
            pltpu.VMEM((tokens, hidden), bf16),
            pltpu.VMEM((tile, hidden), f32),
            pltpu.VMEM((tokens, width), bf16),
            pltpu.VMEM((tokens, width), bf16),
            pltpu.VMEM((tokens, width), bf16),
            pltpu.SemaphoreType.DMA((2 + fold,)),
        ],
        compiler_params=pltpu.CompilerParams(vmem_limit_bytes=VMEM_BYTES),
        cost_estimate=pl.CostEstimate(
            flops=6 * tokens * width * (2 * hidden + width),
            bytes_accessed=8 * width * (2 * hidden + width),
            transcendentals=2 * tokens * hidden,
        ),
        name="dense",
    )(spot, kept, given, inputs, top, vector_rows, hidden_offset, weights)


def table_kernel(sizes, *refs):
    counts, half, line_count = sizes
    chunks = len(counts)
    spot_ref = refs[0]
    pieces = refs[1 : 1 + sum(counts)]
    refs = refs[1 + sum(counts) :]
    pair_grads = refs[:chunks]
    query_grads = refs[chunks : chunks + 2]
    dense_ref, hidden_ref = refs[chunks + 2 : chunks + 4]
    out_ref, total_ref, line_ref, rows_ref, grads_ref, query_ref, sems = refs[chunks + 4 :]
    core = spot_ref[1]
    width = rows_ref.shape[2]
    f32 = jnp.float32

    def fetch(n):
        slot = n % 2
        copies = []
        low = 0
        for piece in pieces[sum(counts[:n]) : sum(counts[: n + 1])]:
            target = rows_ref.at[slot, pl.ds(low, piece.shape[0])]
            copies.append(pltpu.make_async_copy(piece, target, sems.at[slot, len(copies)]))
            low += piece.shape[0]
        copies.append(pltpu.make_async_copy(pair_grads[n], grads_ref.at[slot], sems.at[slot, 2]))
        if n < 2:
            copies.append(
                pltpu.make_async_copy(query_grads[n], query_ref.at[slot], sems.at[slot, 3])
            )
        for copy in copies:
            copy.start()
        return copies

    line_ref[...] = jnp.zeros_like(line_ref)
    waiting = fetch(0)
    step = 384
    for n in range(chunks):
        following = fetch(n + 1) if n + 1 < chunks else []
        for copy in waiting:
            copy.wait()
        slot = n % 2
        for row in range(0, width, step):
            rows = rows_ref[slot, :, row : row + step]
            here = slice(row, row + step)
            for column in range(0, 2 * half, step):
                there = slice(column, column + step)
                part = lax.dot_general(
                    rows, grads_ref[slot, :, there], TN, preferred_element_type=f32
                )
                total_ref[here, there] = part if n == 0 else total_ref[here, there] + part
            if n < 2:
                there = slice(2 * half, 3 * half)
                part = lax.dot_general(rows, query_ref[slot], TN, preferred_element_type=f32)
                total_ref[here, there] = part if n == 0 else total_ref[here, there] + part
        line_ref[pl.ds(0, 1), :] += jnp.sum(
            grads_ref[slot, :, half:].astype(f32), axis=0, keepdims=True
        )
        if n < 2:
            line_ref[pl.ds(1, 1), :] += jnp.sum(
                query_ref[slot].astype(f32), axis=0, keepdims=True
            )
        waiting = following
    columns = 3 * half
    for row in range(0, width, step):
        out_ref[row : row + step, :columns] = total_ref[row : row + step, :].astype(jnp.bfloat16)
    low_core = lax.broadcasted_iota(jnp.int32, (8, width), 1) < half
    mine = low_core == (core == 0)
    halves = jnp.where(mine, jnp.concatenate([line_ref[...], line_ref[...]], axis=1), 0.0)
    vectors = [halves[1:2], halves[0:1], dense_ref[2:8, :]]
    for low in range(0, hidden_ref.shape[1], width):
        vectors.append(hidden_ref[:, low : low + width])
    wide = jnp.concatenate(vectors, axis=0)
    high = wide.astype(jnp.bfloat16).astype(f32)
    pad = jnp.zeros((128 - 2 * line_count, width), f32)
    packed = jnp.concatenate([high, wide - high, pad], axis=0)
    out_ref[:, columns:] = packed.T.astype(jnp.bfloat16)


def table_grads(spot, rows_in, pair_grads, query_grads, dense_lines, hidden_line):
    smem = pl.BlockSpec(memory_space=pltpu.SMEM)
    vmem = pl.BlockSpec(memory_space=pltpu.VMEM)
    hbm = pl.BlockSpec(memory_space=pl.ANY)
    counts = tuple(len(pieces) for pieces in rows_in)
    flat = [piece for pieces in rows_in for piece in pieces]
    rows, total = pair_grads[0].shape
    half = total // 2
    width = flat[0].shape[1]
    bf16 = jnp.bfloat16
    shape = jax.ShapeDtypeStruct
    return pl.pallas_call(
        functools.partial(table_kernel, (counts, half, 8 + hidden_line.shape[1] // width)),
        out_shape=shape((width, 3 * half + 128), bf16),
        in_specs=[smem] + [hbm] * (len(flat) + len(pair_grads) + 2) + [vmem] * 2,
        out_specs=vmem,
        scratch_shapes=[
            pltpu.VMEM((width, 3 * half), jnp.float32),
            pltpu.VMEM((8, half), jnp.float32),
            pltpu.VMEM((2, rows, width), bf16),
            pltpu.VMEM((2, rows, total), bf16),
            pltpu.VMEM((2, rows, half), bf16),
            pltpu.SemaphoreType.DMA((2, 4)),
        ],
        compiler_params=pltpu.CompilerParams(vmem_limit_bytes=VMEM_BYTES),
        cost_estimate=pl.CostEstimate(flops=10**10, bytes_accessed=4 * 10**7, transcendentals=0),
        name="table_grads",
    )(spot, *flat, *pair_grads, *query_grads, dense_lines, hidden_line)


def pick(flag, first, second):
    return jnp.where(flag == 0, first, second)


def split_low(wide, width):
    high = lax.reduce_precision(wide, 8, 7)
    parts = [high.astype(jnp.bfloat16), (wide - high).astype(jnp.bfloat16)]
    pad = width - 2 * wide.shape[-1]
    parts.append(jnp.zeros(wide.shape[:-1] + (pad,), jnp.bfloat16))
    return jnp.concatenate(parts, axis=-1)


def join_low(packed, count):
    wide = packed.astype(jnp.float32)
    return wide[..., :count] + wide[..., count : 2 * count]


def body(
    tokens_in,
    query_weight,
    query_bias,
    key_weight,
    value_weight,
    value_bias,
    mixer_weight,
    mixer_bias,
    first_gain,
    first_shift,
    expand_weight,
    expand_bias,
    shrink_weight,
    shrink_bias,
    second_gain,
    second_shift,
    doc_starts,
    random_blocks,
    cotangent,
):
    f32 = jnp.float32
    bf16 = jnp.bfloat16
    axes = ("head", "blk")
    head_count = lax.axis_size("head")
    cycle_size = lax.axis_size("blk")
    devices = head_count * cycle_size
    head_index = lax.axis_index("head")
    cycle_index = lax.axis_index("blk")
    side = head_index // 2
    core = head_index % 2
    level = cycle_index // 2
    turn = cycle_index % 2
    levels = cycle_size // 2
    local_rows = tokens_in.shape[1]
    model_width = tokens_in.shape[2]
    half_width = model_width // 2
    hidden = expand_weight.shape[1]
    fold = hidden // model_width
    own_rows = query_weight.shape[0]
    part_blocks = local_rows // BLOCK
    half_blocks = 2 * part_blocks
    total_blocks = part_blocks * devices
    slots = 3 + random_blocks.shape[1] + 2 * (GLOBAL_BLOCKS + 1)
    few = slots - GLOBAL_BLOCKS - 1
    groups = ((0, 4), (4 * HEAD_DIM, 2))

    def flat(head, cycle):
        return head * cycle_size + cycle

    everywhere = [(h, b) for h in range(head_count) for b in range(cycle_size)]
    over_side = [(flat(h, b), flat(h ^ 2, b)) for h, b in everywhere]
    over_core = [(flat(h, b), flat(h ^ 1, b)) for h, b in everywhere]
    over_turn = [(flat(h, b), flat(h, b ^ 1)) for h, b in everywhere]
    inward = [
        (flat(h, b), flat(h, b + (1 if h >= 2 else -1)))
        for h, b in everywhere
        if 0 <= b + (1 if h >= 2 else -1) < cycle_size
    ]
    outward = [
        (flat(h, b), flat(h, b + (-1 if h >= 2 else 1)))
        for h, b in everywhere
        if 0 <= b + (-1 if h >= 2 else 1) < cycle_size
    ]

    def send(array, pairs):
        return lax.ppermute(array, axes, pairs)

    def send_back(array, pairs):
        return lax.ppermute(array, axes, [(b, a) for a, b in pairs])

    together = lax.optimization_barrier

    half_index = 2 * cycle_index + side
    spot = jnp.stack([side, core, half_index]).astype(jnp.int32)

    vectors = [
        query_bias,
        value_bias,
        mixer_bias,
        first_gain,
        first_shift,
        shrink_bias,
        second_gain,
        second_shift,
    ]
    line_count = len(vectors) + fold
    line_width = 128
    per_row = -(-(len(vectors) + 1) // own_rows)
    gap = line_width // per_row
    shard = pack(
        key_weight, value_weight, query_weight, vectors + [expand_bias], per_row, gap
    )
    trio = 3 * half_width
    wide_columns = hidden + model_width
    rest_shard = jnp.concatenate(
        [
            expand_weight.reshape(own_rows, model_width, fold)
            .transpose(0, 2, 1)
            .reshape(own_rows, hidden),
            mixer_weight,
            shrink_weight.reshape(own_rows, hidden),
        ],
        axis=1,
    ).astype(bf16)

    latest = []

    def turn_for(array):
        return together((array, latest[-1]))[0] if latest else array

    def mark(array):
        latest.append(array)
        return array

    def done(array):
        return mark(turn_for(array))

    inputs = tokens_in[0]
    beside = send(inputs, over_side)
    near = send(inputs, inward)
    tables = lax.all_gather(shard, axes, axis=0, tiled=True)
    rest = lax.all_gather(together((rest_shard, shard))[0], axes, axis=0, tiled=True)
    inputs_other = send(inputs, over_core)
    inputs_other = done(inputs_other)
    near = done(near)
    passed = send(near, over_side)
    far = send(together((inputs, near))[0], outward)
    beside = done(beside)
    near_other = send(near, over_core)
    near_other = done(near_other)
    beside_other = send(together((beside, near_other))[0], over_core)
    beside_other = done(beside_other)
    tables = done(tables)
    table = jnp.concatenate(
        [pick(core, tables[:, :trio], tables[:, trio : 2 * trio]), tables[:, 2 * trio :]], axis=1
    )

    pair_matrix = table[:, :model_width]
    query_matrix = table[:, model_width:trio]
    every_line = table[:, trio:].astype(f32).reshape(devices, own_rows, line_width)

    def line_of(n, size):
        low = n % per_row * gap
        return every_line[:, n // per_row, low : low + size].reshape(devices * size)

    vector_rows = jnp.stack([line_of(n, own_rows) for n in range(len(vectors))])
    expand_offset = line_of(len(vectors), own_rows * fold)
    expand_offset = expand_offset.reshape(model_width, fold).T.reshape(1, hidden)
    query_offset = pick(core, vector_rows[0, :half_width], vector_rows[0, half_width:])
    value_offset = pick(core, vector_rows[1, :half_width], vector_rows[1, half_width:])
    pair_offset = jnp.concatenate([jnp.zeros((half_width,), f32), value_offset])
    picks = jnp.concatenate(
        [
            lax.dynamic_slice_in_dim(random_blocks, head_index * part_blocks, part_blocks),
            lax.dynamic_slice_in_dim(random_blocks, (head_index ^ 1) * part_blocks, part_blocks),
        ],
        axis=0,
    ).T
    picks = jnp.pad(picks, ((0, 0), (0, 2 * BLOCK - half_blocks)))
    lists = key_lists(
        spot, doc_starts, picks, part_blocks, total_blocks, slots, random_blocks.shape[1]
    )

    def project(rows, matrix, offset):
        return (jnp.dot(rows, matrix, preferred_element_type=f32) + offset).astype(bf16)

    def project_pair(rows):
        return project(rows, pair_matrix, pair_offset)

    query_rows = jnp.concatenate(
        [project(turn_for(rows), query_matrix, query_offset) for rows in (inputs, inputs_other)],
        axis=0,
    ) * jnp.asarray(HEAD_DIM**-0.5, bf16)
    mark(query_rows)
    rows_in = [[inputs], [inputs_other], [beside], [beside_other], [near], [near_other]]
    chunks = [mark(project_pair(turn_for(rows))) for (rows,) in rows_in]
    passed = done(passed)
    passed_other = send(passed, over_core)
    far = done(far)
    far_other = send(far, over_core)
    chunks.append(mark(project_pair(turn_for(passed))))
    passed_other = done(passed_other)
    chunks.append(mark(project_pair(passed_other)))
    chunks.append(mark(project_pair(turn_for(far))))
    far_other = done(far_other)
    chunks.append(mark(project_pair(far_other)))
    rows_in += [[passed], [passed_other], [far], [far_other]]
    mixed_kept, mixed_leaving = attend(lists, query_rows, chunks, groups, slots, few)
    mark(mixed_leaving)
    mixed_given = send(mixed_leaving, over_core)
    (
        layer_out,
        grad_first,
        grad_kept,
        grad_leaving,
        dense_lines,
        hidden_line,
        rest_grad,
    ) = dense(
        spot,
        mixed_kept,
        mixed_given,
        inputs,
        cotangent[0],
        vector_rows,
        expand_offset,
        rest,
    )
    mark(grad_leaving)
    grad_given = send(grad_leaving, over_core)
    rest_total = lax.psum_scatter(rest_grad, axes, scatter_dimension=0, tiled=True)
    pair_grads = attend_back(
        lists, query_rows, (grad_kept, grad_given), chunks, groups, slots, few
    )
    query_grads = pair_grads[:2]
    pair_grads = pair_grads[2:]

    mark(query_grads[0])

    def back(grad, matrix):
        return jnp.einsum("te,de->td", turn_for(grad), matrix, preferred_element_type=f32)

    def leave(n):
        total = back(pair_grads[2 * n + 1], pair_matrix)
        if n == 0:
            total = total + back(query_grads[1], query_matrix)
        return send(mark(total.astype(bf16)), over_core)

    def stay(n, *extras):
        total = back(pair_grads[2 * n], pair_matrix)
        for extra in extras:
            total = total + extra.astype(f32)
        return mark(total.astype(bf16))

    passed_given = leave(3)
    far_given = leave(4)
    beside_given = leave(1)
    passed_given = done(passed_given)
    passed_back = send(stay(3, passed_given), over_side)
    near_given = leave(2)
    far_given = done(far_given)
    far_back = send_back(stay(4, far_given), outward)
    near_given = done(near_given)
    beside_given = done(beside_given)
    table_grad = mark(
        table_grads(
            spot,
            rows_in,
            pair_grads,
            [turn_for(grad) for grad in query_grads],
            dense_lines,
            hidden_line,
        )
    )
    by_head = lax.all_to_all(
        table_grad.reshape(head_count, cycle_size * own_rows, trio + line_width),
        "head",
        split_axis=0,
        concat_axis=0,
        tiled=True,
    )
    passed_back = done(passed_back)
    far_back = done(far_back)
    near_back = send_back(stay(2, near_given, passed_back), inward)
    beside_back = send(stay(1, beside_given), over_side)
    own_given = leave(0)
    by_head = done(by_head).reshape(2, 2, cycle_size, own_rows, trio + line_width)
    by_core = jnp.sum(by_head[..., :trio].astype(f32), axis=0).astype(bf16)
    line_sum = jnp.sum(join_low(by_head[..., trio:], line_count), axis=(0, 1))
    packed = mark(
        jnp.concatenate([by_core[0], by_core[1], split_low(line_sum, line_width)], axis=-1)
    )
    arrived = lax.all_to_all(packed, "blk", split_axis=0, concat_axis=0, tiled=True)
    own_given = done(own_given)
    own_total = mark(
        grad_first
        + back(pair_grads[0], pair_matrix)
        + back(query_grads[0], query_matrix)
        + own_given.astype(f32)
        + far_back.astype(f32)
    )
    near_back = done(near_back)
    arrived = done(arrived)
    table_own = jnp.sum(arrived[..., : 2 * trio].astype(f32), axis=0)
    line_own = jnp.sum(join_low(arrived[..., 2 * trio :], line_count), axis=0)
    rest_total = rest_total.astype(f32)
    input_grad = own_total + beside_back.astype(f32) + near_back.astype(f32)

    def columns_of(which):
        low = which * half_width
        return jnp.concatenate(
            [table_own[:, at : at + half_width] for at in (low, trio + low)], axis=1
        )

    return (
        layer_out[None],
        input_grad[None],
        columns_of(2),
        line_own[:, 0],
        columns_of(0),
        columns_of(1),
        line_own[:, 1],
        rest_total[:, hidden:wide_columns],
        line_own[:, 2],
        line_own[:, 3],
        line_own[:, 4],
        rest_total[:, :hidden]
        .reshape(own_rows, fold, model_width)
        .transpose(0, 2, 1)
        .reshape(own_rows, hidden),
        line_own[:, len(vectors) :].reshape(-1),
        rest_total[:, wide_columns:].reshape(own_rows * fold, model_width),
        line_own[:, 5],
        line_own[:, 6],
        line_own[:, 7],
    )


def solution(mesh):
    in_specs = (
        P("blk", "head", None),
        P(("head", "blk"), None),
        P(("head", "blk")),
        P(("head", "blk"), None),
        P(("head", "blk"), None),
        P(("head", "blk")),
        P(("head", "blk"), None),
        P(("head", "blk")),
        P(("head", "blk")),
        P(("head", "blk")),
        P(("head", "blk"), None),
        P(("head", "blk")),
        P(("head", "blk"), None),
        P(("head", "blk")),
        P(("head", "blk")),
        P(("head", "blk")),
        P(),
        P("blk", None),
        P("blk", "head", None),
    )
    out_specs = (
        P("blk", "head", None),
        P("blk", "head", None),
        P(("head", "blk"), None),
        P(("head", "blk")),
        P(("head", "blk"), None),
        P(("head", "blk"), None),
        P(("head", "blk")),
        P(("head", "blk"), None),
        P(("head", "blk")),
        P(("head", "blk")),
        P(("head", "blk")),
        P(("head", "blk"), None),
        P(("head", "blk")),
        P(("head", "blk"), None),
        P(("head", "blk")),
        P(("head", "blk")),
        P(("head", "blk")),
    )
    return jax.shard_map(body, mesh=mesh, in_specs=in_specs, out_specs=out_specs, check_vma=False)
```
